256 devices in a mesh: dp: 256 (over y, z, x, core).
Axes of the slice: x: 4, y: 4, z: 8, core: 2. Of those that a mesh axis runs over, the one named last changes fastest.
Arguments:
- images: bfloat16 [1048576, 256], P('dp'), may hold values from -8 to 8
- landmarks: bfloat16 [512, 256], replicated, may hold values from -6 to 6
Outputs:
- q_factor: float32 [1048576, 512], P('dp')
- r_factor: float32 [512, 512], replicated
The draws below stay inside these ranges and needn't reach their ends.
All inputs are finite; a program needn't handle non-finite values.
Results may differ from the reference program's by a relative error of at most 0.0003.
Values sent between devices are 32-bit elements; how exact they have to be, the bound alone decides.
A program may use at most 128 MiB of HBM per device.

```python
import math
import jax
import jax.numpy as jnp
from jax import lax

IMG = 256
LM = 512
ROW_DEV = 4096
ROWS = 1048576
N_DP = 256


def draw_images(key, part):
    key = jax.random.fold_in(key, 11)
    noise_key, direction_key, jitter_key = jax.random.split(key, 3)
    block_rows = min(256, ROW_DEV)
    block_count = ROWS // block_rows
    position = jnp.arange(block_count, dtype=jnp.float32) / block_count
    jitter = jax.random.uniform(jitter_key, (block_count, 1), jnp.float32, 0.8, 1.25)
    directions = jax.random.normal(direction_key, (block_count, IMG), jnp.float32)
    noise = jax.random.normal(noise_key, (ROWS, IMG), jnp.float32)
    strength = (0.6 + 0.9 * position)[:, None] * jitter
    offsets = strength * directions
    values = noise.reshape(block_count, block_rows, IMG) + offsets[:, None, :]
    return jnp.clip(values, -8.0, 8.0).reshape(ROWS, IMG).astype(jnp.bfloat16)


def scatter_about(rng, shape, spread, limit, held_as=jnp.bfloat16):
    array = jax.random.normal(rng, shape, jnp.float32) * spread
    return jnp.minimum(jnp.maximum(array, -limit), limit).astype(held_as)


def setup_inputs(seed: int = 0) -> dict:
    streams_of = jax.random.split(jax.random.key(seed), 3)
    return {
        "images": draw_images(jax.random.fold_in(streams_of[2], 71), 0),
        "landmarks": scatter_about(streams_of[1], (LM, IMG), 1.0, 6.0),
    }


EPSILON = 1e-05
PRECISE = lax.Precision.HIGHEST

def features(images, landmarks):
    products = jnp.dot(images.astype(jnp.float32), landmarks.T.astype(jnp.float32), preferred_element_type=jnp.float32)
    pixels = images.astype(jnp.float32)
    row_scale = lax.rsqrt(lax.optimization_barrier(jnp.mean(pixels * pixels, axis=1)) + EPSILON)
    landmark_f = landmarks.astype(jnp.float32)
    land_scale = lax.rsqrt(lax.optimization_barrier(jnp.mean(landmark_f * landmark_f, axis=1)) + EPSILON)
    cosine = products * row_scale[:, None] * land_scale[None, :] / IMG
    return jnp.exp(math.sqrt(IMG) * cosine)

def factor_pair(gram):
    order = gram.shape[0]
    lower = jnp.linalg.cholesky(gram)
    identity = jnp.eye(order, dtype=gram.dtype)
    inverse = jax.scipy.linalg.solve_triangular(lower, identity, lower=True)
    return (lower.T, inverse.T)

def reference(images, landmarks):
    slab_rows = images.reshape(N_DP, ROW_DEV, IMG)

    def add_block(running, slab):
        kernel_cols = features(slab, landmarks)
        square = jnp.dot(kernel_cols.T.astype(jnp.float32), kernel_cols.astype(jnp.float32), precision=PRECISE, preferred_element_type=jnp.float32)
        return (running + square, None)
    gram, _ = lax.scan(add_block, jnp.zeros((LM, LM), jnp.float32), slab_rows)
    upper_factor, inverse = factor_pair(gram)
    total_rows = N_DP * ROW_DEV

    def solve_block(slab):
        kernel_cols = features(slab, landmarks)
        return jnp.dot(kernel_cols.astype(jnp.float32), inverse.astype(jnp.float32), precision=PRECISE, preferred_element_type=jnp.float32) * math.sqrt(total_rows)
    scaled_q = lax.map(solve_block, slab_rows).reshape(total_rows, LM)
    return (scaled_q, upper_factor / math.sqrt(total_rows))
```

```python
import functools
import math

import jax
import jax.numpy as jnp
from jax import lax
from jax.experimental import pallas as pl
from jax.experimental.pallas import tpu as pltpu
from jax.sharding import PartitionSpec as P

MESH = pl.DeviceIdType.MESH
NX, NY, NZ = 4, 4, 8
NXY = NX*NY

def dev(y, z, x, c):
    return ((y * NZ + z) * NX + x) * 2 + c

def comm_kernel(chunks, g_ref, o_ref, crecv, half, rsbuf, zbuf, part,
                c_ss, c_rs, rs_ss, rs_rs, z_ss, z_rs, ag_ss, ag_rs, f_ss, f_rs):
    me = lax.axis_index("dp")
    c = me % 2
    x = (me // 2) % NX
    z = (me // (2 * NX)) % NZ
    y = me // (2 * NX * NZ)
    sib = dev(y, z, x, 1 - c)
    def xy_peer(rel):
        px = (x + rel % NX) % NX
        py = (y + rel // NX) % NY
        return py * NX + px, dev(py, z, px, c)
    def xy_from(rel):
        px = (x + NX - rel % NX) % NX
        py = (y + NY - rel // NX) % NY
        return py * NX + px
    def z_peer(rel):
        return dev(y, (z + rel) % NZ, x, c)
    def sl(off, n):
        return pl.ds(pl.multiple_of(off, 8), n)
    bar = pltpu.get_barrier_semaphore()
    def sig(d):
        pl.semaphore_signal(bar, inc=1, device_id=(d,), device_id_type=MESH)
    sig(sib)
    @pl.loop(1, NXY)
    def _(r):
        sig(xy_peer(r)[1])
    @pl.loop(1, NZ)
    def _(r):
        sig(z_peer(r))
    pl.semaphore_wait(bar, 1 + NXY - 1 + NZ - 1)

    mine = y * NX + x
    C = []
    off = 0
    for k, rows in enumerate(chunks):
        C.append((k, off, rows // 2, rows // 32, off // 2, off // 32))
        off += rows
    def core_copy(k, off, h, p, ho, po):
        return pltpu.make_async_remote_copy(g_ref.at[sl(off + (1 - c) * h, h)], crecv.at[pl.ds(ho, h)],
            c_ss.at[k], c_rs.at[k], device_id=(sib,), device_id_type=MESH)
    def rs_copy(ch, rel):
        k, off, h, p, ho, po = ch
        idx, d = xy_peer(rel)
        return pltpu.make_async_remote_copy(half.at[sl(ho + idx * p, p)], rsbuf.at[sl(ho + rel * p, p)],
            rs_ss.at[k, rel], rs_rs.at[k, rel], device_id=(d,), device_id_type=MESH)
    def z_copy(ch, rel):
        k, off, h, p, ho, po = ch
        return pltpu.make_async_remote_copy(part.at[pl.ds(po, p)], zbuf.at[z, pl.ds(po, p)],
            z_ss.at[k, rel], z_rs.at[k, rel], device_id=(z_peer(rel),), device_id_type=MESH)
    def ag_copy(ch, rel):
        k, off, h, p, ho, po = ch
        idx, d = xy_peer(rel)
        src = o_ref.at[sl(off + c * h + mine * p, p)]
        return pltpu.make_async_remote_copy(src, src, ag_ss.at[k, rel], ag_rs.at[k, rel], device_id=(d,), device_id_type=MESH)
    def fwd_copy(ch, rel):
        k, off, h, p, ho, po = ch
        idx = xy_from(rel)
        src = o_ref.at[sl(off + c * h + idx * p, p)]
        return pltpu.make_async_remote_copy(src, src, f_ss.at[k, rel], f_rs.at[k, rel], device_id=(sib,), device_id_type=MESH)
    for ch in C:
        core_copy(*ch).start()
    for ch in C:
        k, off, h, p, ho, po = ch
        core_copy(*ch).wait_recv()
        half[pl.ds(ho, h)] = g_ref[sl(off + c * h, h)] + crecv[pl.ds(ho, h)]
        @pl.loop(1, NXY)
        def _(r):
            rs_copy(ch, r).start()
    for ch in C:
        k, off, h, p, ho, po = ch
        @pl.loop(1, NXY)
        def _(r):
            rs_copy(ch, r).wait_recv()
        acc = half[sl(ho + mine * p, p)]
        for r in range(1, NXY):
            acc = acc + rsbuf[pl.ds(ho + r * p, p)]
        part[pl.ds(po, p)] = acc
        zbuf[z, pl.ds(po, p)] = acc
        @pl.loop(1, NZ)
        def _(r):
            z_copy(ch, r).start()
    for ch in C:
        k, off, h, p, ho, po = ch
        @pl.loop(1, NZ)
        def _(r):
            z_copy(ch, r).wait_recv()
        acc = zbuf[0, pl.ds(po, p)]
        for r in range(1, NZ):
            acc = acc + zbuf[r, pl.ds(po, p)]
        o_ref[sl(off + c * h + mine * p, p)] = acc
        fwd_copy(ch, 0).start()
        @pl.loop(1, NXY)
        def _(r):
            ag_copy(ch, r).start()
    for ch in C:
        @pl.loop(1, NXY)
        def _(r):
            ag_copy(ch, r).wait_recv()
            fwd_copy(ch, r).start()
    for ch in C:
        @pl.loop(0, NXY)
        def _(r):
            k, off, h, p, ho, po = ch
            idx = xy_from(r)
            dst = o_ref.at[sl(off + (1 - c) * h + idx * p, p)]
            pltpu.make_async_remote_copy(dst, dst, f_ss.at[k, r], f_rs.at[k, r], device_id=(sib,), device_id_type=MESH).wait_recv()
    for ch in C:
        core_copy(*ch).wait_send()
        fwd_copy(ch, 0).wait_send()
        @pl.loop(1, NXY)
        def _(r):
            rs_copy(ch, r).wait_send()
            ag_copy(ch, r).wait_send()
            fwd_copy(ch, r).wait_send()
        @pl.loop(1, NZ)
        def _(r):
            z_copy(ch, r).wait_send()

def comm(g, chunks=(512, 768), cid=0):
    rows = g.shape[0]
    nc = len(chunks)
    D = pltpu.SemaphoreType.DMA
    return pl.pallas_call(
        functools.partial(comm_kernel, chunks),
        out_shape=jax.ShapeDtypeStruct((rows, 128), jnp.float32),
        in_specs=[pl.BlockSpec(memory_space=pltpu.VMEM)],
        out_specs=pl.BlockSpec(memory_space=pltpu.VMEM),
        scratch_shapes=[
            pltpu.VMEM((rows // 2, 128), jnp.float32),
            pltpu.VMEM((rows // 2, 128), jnp.float32),
            pltpu.VMEM((rows // 2, 128), jnp.float32),
            pltpu.VMEM((NZ, rows // 32, 128), jnp.float32),
            pltpu.VMEM((rows // 32, 128), jnp.float32),
            D((nc,)), D((nc,)), D((nc, NXY)), D((nc, NXY)), D((nc, NZ)), D((nc, NZ)),
            D((nc, NXY)), D((nc, NXY)), D((nc, NXY)), D((nc, NXY)),
        ],
        compiler_params=pltpu.CompilerParams(collective_id=cid, has_side_effects=True),
        name="gram_all_reduce",
    )(g)

F32 = jnp.float32
HI = lax.Precision.HIGHEST
BLK = {}
n = 0
for i in range(4):
    for j in range(i, 4):
        BLK[i, j] = n; n += 1

def mm(a, b):
    return lax.dot_general(a, b, (((1,), (0,)), ((), ())), precision=HI, preferred_element_type=F32)
def mtm(a, b):
    return lax.dot_general(a, b, (((0,), (0,)), ((), ())), precision=HI, preferred_element_type=F32)

def lane_splat(v, c):
    return jnp.broadcast_to(v[:, c:c + 1], (8, 128))
def row_splat(v, r):
    return jnp.broadcast_to(v[r:r + 1, :], (8, 128))

def tsum(xs):
    xs = list(xs)
    while len(xs) > 1:
        xs = [xs[i] + xs[i + 1] if i + 1 < len(xs) else xs[i] for i in range(0, len(xs), 2)]
    return xs[0]

def small_factor(a):
    l = [[None] * 8 for _ in range(8)]
    s = [None] * 8
    for j in range(8):
        s[j] = lax.rsqrt(a[j][j])
        for i in range(j + 1, 8):
            l[i][j] = a[i][j] * s[j]
        for i in range(j + 1, 8):
            for k in range(j + 1, i + 1):
                a[i][k] = a[i][k] - l[i][j] * l[k][j]
    w = [[None] * 8 for _ in range(8)]
    for j in range(8):
        w[j][j] = s[j]
        for i in range(j + 1, 8):
            w[i][j] = -s[i] * tsum([l[i][k] * w[k][j] for k in range(j, i)])
    return w

def diag_inverse(A):
    lane = lax.broadcasted_iota(jnp.int32, (8, 128), 1)
    sub = lax.broadcasted_iota(jnp.int32, (8, 128), 0)
    A = list(A)
    out = []
    for p in range(16):
        c0 = 8 * p
        P = A[p]
        cols = [lane_splat(P, c0 + j) for j in range(8)]
        a = [[row_splat(cols[j], i) if j <= i else None for j in range(8)] for i in range(8)]
        w = small_factor(a)
        inpanel = (lane >= c0) & (lane < c0 + 8)
        T = jnp.where(inpanel, (lane - c0 == sub).astype(F32), P)
        Tb = [row_splat(T, j) for j in range(8)]
        V = [tsum([w[i][j] * Tb[j] for j in range(i + 1)]) for i in range(8)]
        packed = V[0]
        for i in range(1, 8):
            packed = jnp.where(sub == i, V[i], packed)
        out.append(packed)
        if p < 15:
            Y = [tsum([w[i][j] * V[i] for i in range(j, 8)]) for j in range(8)]
            for q in range(p + 1, 16):
                m = [lane_splat(A[q], c0 + j) for j in range(8)]
                base = jnp.where(inpanel, 0.0, A[q])
                A[q] = base - tsum([m[j] * Y[j] for j in range(8)])
    row = [jnp.where(lane <= sub + 8 * p, out[p], 0.0) for p in range(16)]
    return row

def chol_kernel(g_ref, r_ref, hi_ref, lo_ref):
    n_rows = 1.0 / 1048576.0
    A = {k: g_ref[128 * v:128 * v + 128, :] * n_rows for k, v in BLK.items()}
    X = {}
    Bt = {}
    for k in range(4):
        strips = diag_inverse([A[k, k][8 * p:8 * p + 8, :] for p in range(16)])
        W = jnp.concatenate(strips, axis=0)
        U = {j: mm(W, A[k, j]) for j in range(k, 4)}
        for j in range(k + 1, 4):
            for i in range(k + 1, j + 1):
                A[i, j] = A[i, j] - mtm(U[i], U[j])
        X[k, k] = W
        for m in range(k):
            X[k, m] = mm(W, Bt[k, m])
        for i in range(k + 1, 4):
            for m in range(k + 1):
                t = mtm(U[i], X[k, m])
                Bt[i, m] = -t if m == k else Bt[i, m] - t
        rr = lax.broadcasted_iota(jnp.int32, (128, 128), 0)
        cc = lax.broadcasted_iota(jnp.int32, (128, 128), 1)
        for j in range(4):
            blk = jnp.zeros((128, 128), F32) if j < k else (jnp.where(rr <= cc, U[k], 0.0) if j == k else U[j])
            r_ref[128 * k:128 * k + 128, 128 * j:128 * j + 128] = blk
        for m in range(4):
            blk = X[k, m].T if m <= k else jnp.zeros((128, 128), F32)
            h = blk.astype(jnp.bfloat16)
            hi_ref[128 * m:128 * m + 128, 128 * k:128 * k + 128] = h
            lo_ref[128 * m:128 * m + 128, 128 * k:128 * k + 128] = (blk - h.astype(F32)).astype(jnp.bfloat16)

def chol(g):
    V = pl.BlockSpec(memory_space=pltpu.VMEM)
    return pl.pallas_call(chol_kernel,
        out_shape=(jax.ShapeDtypeStruct((512, 512), F32), jax.ShapeDtypeStruct((512, 512), jnp.bfloat16), jax.ShapeDtypeStruct((512, 512), jnp.bfloat16)),
        in_specs=[V], out_specs=(V, V, V),
        compiler_params=pltpu.CompilerParams(vmem_limit_bytes=40 << 20), name="factor")(g)

F32 = jnp.float32
BF = jnp.bfloat16
EPS = 1e-5
TILE = 512

def dot_t(a, b):
    return lax.dot_general(a, b, (((1,), (1,)), ((), ())), preferred_element_type=F32)
def t_dot(a, b):
    return lax.dot_general(a, b, (((0,), (0,)), ((), ())), preferred_element_type=F32)

def feat_kernel(steps, x_ref, lm_ref, ls_ref, hi_ref, lo_ref, g_ref, acc0, acc1, acc2):
    i = pl.program_id(0)
    x = x_ref[...]
    prod = dot_t(x, lm_ref[...])
    xf = x.astype(F32)
    rs = lax.rsqrt(jnp.mean(xf * xf, axis=1, keepdims=True) + EPS)
    k = jnp.exp2(prod * rs * ls_ref[0:1, :])
    hi = k.astype(BF)
    lo = (k - hi.astype(F32)).astype(BF)
    hi_ref[...] = hi
    lo_ref[...] = lo
    p0 = t_dot(hi[:, :256], jnp.concatenate([hi, lo], axis=1))
    p1 = t_dot(hi[:, 256:], jnp.concatenate([hi[:, 256:], lo[:, 256:]], axis=1))
    p2 = t_dot(lo[:, :256], hi[:, 256:])
    @pl.when(i == 0)
    def _():
        acc0[...] = p0
        acc1[...] = p1
        acc2[...] = p2
    @pl.when(i > 0)
    def _():
        acc0[...] += p0
        acc1[...] += p1
        acc2[...] += p2
    @pl.when(i == steps - 1)
    def _():
        c0 = acc0[:, 512:768]
        g00 = acc0[:, :256] + (c0 + c0.T)
        g01 = acc0[:, 256:512] + (acc0[:, 768:] + acc2[...])
        c1 = acc1[:, 256:]
        g11 = acc1[:, :256] + (c1 + c1.T)
        blocks = [g00[:128, :128], g00[:128, 128:], g01[:128, :128], g01[:128, 128:],
                  g00[128:, 128:], g01[128:, :128], g01[128:, 128:],
                  g11[:128, :128], g11[:128, 128:], g11[128:, 128:]]
        for n, b in enumerate(blocks):
            g_ref[128 * n:128 * n + 128, :] = b

def feat(x, lm, tile=TILE):
    rows = x.shape[0]
    steps = rows // tile
    lf = lm.astype(F32)
    ls = lax.rsqrt(jnp.mean(lf * lf, axis=1) + EPS) * (math.log2(math.e) / math.sqrt(x.shape[1]))
    ls = jnp.broadcast_to(ls[None, :], (8, 512))
    return pl.pallas_call(functools.partial(feat_kernel, steps), grid=(steps,),
        in_specs=[pl.BlockSpec((tile, 256), lambda i: (i, 0)), pl.BlockSpec((512, 256), lambda i: (0, 0)), pl.BlockSpec((8, 512), lambda i: (0, 0))],
        out_specs=(pl.BlockSpec((tile, 512), lambda i: (i, 0)), pl.BlockSpec((tile, 512), lambda i: (i, 0)), pl.BlockSpec((1280, 128), lambda i: (0, 0))),
        out_shape=(jax.ShapeDtypeStruct((rows, 512), BF), jax.ShapeDtypeStruct((rows, 512), BF), jax.ShapeDtypeStruct((1280, 128), F32)),
        scratch_shapes=[pltpu.VMEM((256, 1024), F32), pltpu.VMEM((256, 512), F32), pltpu.VMEM((256, 256), F32)],
        compiler_params=pltpu.CompilerParams(vmem_limit_bytes=40 << 20), name="features")(x, lm, ls)

def dot(a, b):
    return lax.dot_general(a, b, (((1,), (0,)), ((), ())), preferred_element_type=F32)

def q_kernel(hi_ref, lo_ref, rh_ref, rl_ref, q_ref):
    hi = hi_ref[...]
    lo = lo_ref[...]
    rh = rh_ref[...]
    rl = rl_ref[...]
    q_ref[:, :256] = dot(hi[:, :256], rh[:256, :256]) + (dot(hi[:, :256], rl[:256, :256]) + dot(lo[:, :256], rh[:256, :256]))
    q_ref[:, 256:] = dot(hi, rh[:, 256:]) + (dot(hi, rl[:, 256:]) + dot(lo, rh[:, 256:]))

def qmul(hi, lo, rh, rl, tile=TILE):
    rows = hi.shape[0]
    row = pl.BlockSpec((tile, 512), lambda i: (i, 0))
    whole = pl.BlockSpec((512, 512), lambda i: (0, 0))
    return pl.pallas_call(q_kernel, grid=(rows // tile,), in_specs=[row, row, whole, whole], out_specs=row,
        out_shape=jax.ShapeDtypeStruct((rows, 512), F32),
        compiler_params=pltpu.CompilerParams(vmem_limit_bytes=40 << 20), name="q_product")(hi, lo, rh, rl)


def local(images, landmarks):
    hi, lo, gram = feat(images, landmarks, 1024)
    summed = comm(gram)
    r, rh, rl = chol(summed)
    return qmul(hi, lo, rh, rl, 1024), r


def solution(mesh):
    in_specs = (P("dp", None), P())
    out_specs = (P("dp", None), P())
    return jax.shard_map(local, mesh=mesh, in_specs=in_specs, out_specs=out_specs, check_vma=False)
```

```python
import functools
import math

import jax
import jax.numpy as jnp
from jax import lax
from jax.experimental import pallas as pl
from jax.experimental.pallas import tpu as pltpu
from jax.sharding import PartitionSpec as P

F32 = jnp.float32
BF = jnp.bfloat16
EPS = 1e-5
HI = lax.Precision.HIGHEST
MESH = pl.DeviceIdType.MESH
NX, NY, NZ = 4, 4, 8
NXY = NX * NY
TILES = 4
CHUNKS = (512, 768)

def dot_t(a, b, precision=None):
    return lax.dot_general(a, b, (((1,), (1,)), ((), ())), precision=precision, preferred_element_type=F32)

def t_dot(a, b):
    return lax.dot_general(a, b, (((0,), (0,)), ((), ())), preferred_element_type=F32)

def dev(y, z, x, c):
    return ((y * NZ + z) * NX + x) * 2 + c

def gram_kernel(x_ref, lm_ref, o_ref, hi_ref, lo_ref, xbuf, hbuf, lbuf, g_ref, acc0, acc2,
                crecv, half, rsbuf, zbuf, part, x_s, h_s, l_s,
                c_ss, c_rs, rs_ss, rs_rs, z_ss, z_rs, ag_ss, ag_rs, f_ss, f_rs):
    me = lax.axis_index("dp")
    c = me % 2
    x = (me // 2) % NX
    z = (me // (2 * NX)) % NZ
    y = me // (2 * NX * NZ)
    sib = dev(y, z, x, 1 - c)
    tile = x_ref.shape[0] // TILES

    def xy_peer(rel):
        px = (x + rel % NX) % NX
        py = (y + rel // NX) % NY
        return py * NX + px, dev(py, z, px, c)

    def xy_from(rel):
        px = (x + NX - rel % NX) % NX
        py = (y + NY - rel // NX) % NY
        return py * NX + px

    def z_peer(rel):
        return dev(y, (z + rel) % NZ, x, c)

    def sl(off, n):
        return pl.ds(pl.multiple_of(off, 8), n)

    def rows(t):
        return pl.ds(t * tile, tile)

    def x_copy(t):
        return pltpu.make_async_copy(x_ref.at[rows(t)], xbuf.at[rows(t)], x_s.at[t])

    def h_copy(t):
        return pltpu.make_async_copy(hbuf.at[rows(t)], hi_ref.at[rows(t)], h_s.at[t])

    def l_copy(t):
        return pltpu.make_async_copy(lbuf.at[rows(t)], lo_ref.at[rows(t)], l_s.at[t])

    for t in range(TILES):
        x_copy(t).start()

    bar = pltpu.get_barrier_semaphore()

    def sig(d):
        pl.semaphore_signal(bar, inc=1, device_id=(d,), device_id_type=MESH)

    sig(sib)

    @pl.loop(1, NXY)
    def _(r):
        sig(xy_peer(r)[1])

    @pl.loop(1, NZ)
    def _(r):
        sig(z_peer(r))

    lf = lm_ref[...].astype(F32)
    ones = jnp.full((8, lf.shape[1]), 1.0 / lf.shape[1], F32)
    ls = lax.rsqrt(dot_t(ones, lf * lf, HI) + EPS)[0:1, :] * (math.log2(math.e) / math.sqrt(lf.shape[1]))

    def features(t):
        xt = xbuf[rows(t), :]
        xf = xt.astype(F32)
        rs = lax.rsqrt(jnp.mean(xf * xf, axis=1, keepdims=True) + EPS)
        k = jnp.exp2(dot_t(xt, lm_ref[...]) * rs * ls)
        hi = k.astype(BF)
        hbuf[rows(t), :] = hi
        lbuf[rows(t), :] = (k - hi.astype(F32)).astype(BF)

    def gram0(t):
        hi = hbuf[rows(t), :]
        lo = lbuf[rows(t), :]
        p0 = t_dot(hi[:, :256], jnp.concatenate([hi, lo], axis=1))
        p2 = t_dot(lo[:, :256], hi[:, 256:])
        if t == 0:
            acc0[...] = p0
            acc2[...] = p2
        else:
            acc0[...] += p0
            acc2[...] += p2

    for t in range(TILES + 1):
        if t < TILES:
            x_copy(t).wait()
            features(t)
        if t > 0:
            h_copy(t - 1).start()
            l_copy(t - 1).start()
            gram0(t - 1)

    def put(n, b):
        g_ref[128 * n:128 * n + 128, :] = b

    cross = acc0[:, 512:768]
    g00 = acc0[:, :256] + (cross + cross.T)
    g01 = acc0[:, 256:512] + (acc0[:, 768:] + acc2[...])
    put(0, g00[:128, :128])
    put(1, g00[:128, 128:])
    put(2, g01[:128, :128])
    put(3, g01[:128, 128:])

    mine = y * NX + x
    C = []
    off = 0
    for k, n in enumerate(CHUNKS):
        C.append((k, off, n // 2, n // 32, off // 2, off // 32))
        off += n

    def core_copy(k, off, h, p, ho, po):
        return pltpu.make_async_remote_copy(
            g_ref.at[sl(off + (1 - c) * h, h)], crecv.at[pl.ds(ho, h)],
            c_ss.at[k], c_rs.at[k], device_id=(sib,), device_id_type=MESH)

    def rs_copy(ch, rel):
        k, off, h, p, ho, po = ch
        idx, d = xy_peer(rel)
        return pltpu.make_async_remote_copy(
            half.at[sl(ho + idx * p, p)], rsbuf.at[sl(ho + rel * p, p)],
            rs_ss.at[k, rel], rs_rs.at[k, rel], device_id=(d,), device_id_type=MESH)

    def z_copy(ch, rel):
        k, off, h, p, ho, po = ch
        return pltpu.make_async_remote_copy(
            part.at[pl.ds(po, p)], zbuf.at[z, pl.ds(po, p)],
            z_ss.at[k, rel], z_rs.at[k, rel], device_id=(z_peer(rel),), device_id_type=MESH)

    def ag_copy(ch, rel):
        k, off, h, p, ho, po = ch
        idx, d = xy_peer(rel)
        src = o_ref.at[sl(off + c * h + mine * p, p)]
        return pltpu.make_async_remote_copy(
            src, src, ag_ss.at[k, rel], ag_rs.at[k, rel], device_id=(d,), device_id_type=MESH)

    def fwd_copy(ch, rel, core):
        k, off, h, p, ho, po = ch
        src = o_ref.at[sl(off + core * h + xy_from(rel) * p, p)]
        return pltpu.make_async_remote_copy(
            src, src, f_ss.at[k, rel], f_rs.at[k, rel], device_id=(sib,), device_id_type=MESH)

    pl.semaphore_wait(bar, 1 + NXY - 1 + NZ - 1)
    core_copy(*C[0]).start()

    put(4, g00[128:, 128:])
    put(5, g01[128:, :128])
    put(6, g01[128:, 128:])
    h1 = hbuf[:, 256:]
    p1 = t_dot(h1, jnp.concatenate([h1, lbuf[:, 256:]], axis=1))
    cross = p1[:, 256:]
    g11 = p1[:, :256] + (cross + cross.T)
    put(7, g11[:128, :128])
    put(8, g11[:128, 128:])
    put(9, g11[128:, 128:])
    core_copy(*C[1]).start()

    for ch in C:
        k, off, h, p, ho, po = ch
        core_copy(*ch).wait_recv()
        half[pl.ds(ho, h)] = g_ref[sl(off + c * h, h)] + crecv[pl.ds(ho, h)]
        for r in range(1, NXY):
            rs_copy(ch, r).start()
    for ch in C:
        k, off, h, p, ho, po = ch

        @pl.loop(1, NXY)
        def _(r):
            rs_copy(ch, r).wait_recv()

        acc = half[sl(ho + mine * p, p)]
        for r in range(1, NXY):
            acc = acc + rsbuf[pl.ds(ho + r * p, p)]
        part[pl.ds(po, p)] = acc
        zbuf[z, pl.ds(po, p)] = acc
        for r in range(1, NZ):
            z_copy(ch, r).start()
    for ch in C:
        k, off, h, p, ho, po = ch

        @pl.loop(1, NZ)
        def _(r):
            z_copy(ch, r).wait_recv()

        acc = zbuf[0, pl.ds(po, p)]
        for r in range(1, NZ):
            acc = acc + zbuf[r, pl.ds(po, p)]
        o_ref[sl(off + c * h + mine * p, p)] = acc
        for r in range(1, NXY):
            ag_copy(ch, r).start()
        fwd_copy(ch, 0, c).start()
    for ch in C:
        @pl.loop(1, NXY)
        def _(r):
            ag_copy(ch, r).wait_recv()
            fwd_copy(ch, r, c).start()
    for ch in C:
        @pl.loop(0, NXY)
        def _(r):
            fwd_copy(ch, r, 1 - c).wait_recv()
    for ch in C:
        core_copy(*ch).wait_send()
        fwd_copy(ch, 0, c).wait_send()

        @pl.loop(1, NXY)
        def _(r):
            rs_copy(ch, r).wait_send()
            ag_copy(ch, r).wait_send()
            fwd_copy(ch, r, c).wait_send()

        @pl.loop(1, NZ)
        def _(r):
            z_copy(ch, r).wait_send()
    for t in range(TILES):
        h_copy(t).wait()
        l_copy(t).wait()

def gram_sum(x, lm):
    rows = x.shape[0]
    g = sum(CHUNKS)
    nc = len(CHUNKS)
    D = pltpu.SemaphoreType.DMA
    VM = pltpu.VMEM
    return pl.pallas_call(
        gram_kernel,
        out_shape=(jax.ShapeDtypeStruct((g, 128), F32), jax.ShapeDtypeStruct((rows, 512), BF), jax.ShapeDtypeStruct((rows, 512), BF)),
        in_specs=[pl.BlockSpec(memory_space=pl.ANY), pl.BlockSpec(memory_space=VM)],
        out_specs=(pl.BlockSpec(memory_space=VM), pl.BlockSpec(memory_space=pl.ANY), pl.BlockSpec(memory_space=pl.ANY)),
        scratch_shapes=[
            VM((rows, 256), BF), VM((rows, 512), BF), VM((rows, 512), BF), VM((g, 128), F32),
            VM((256, 1024), F32), VM((256, 256), F32),
            VM((g // 2, 128), F32), VM((g // 2, 128), F32), VM((g // 2, 128), F32),
            VM((NZ, g // 32, 128), F32), VM((g // 32, 128), F32),
            D((TILES,)), D((TILES,)), D((TILES,)),
            D((nc,)), D((nc,)), D((nc, NXY)), D((nc, NXY)), D((nc, NZ)), D((nc, NZ)),
            D((nc, NXY)), D((nc, NXY)), D((nc, NXY)), D((nc, NXY)),
        ],
        compiler_params=pltpu.CompilerParams(collective_id=0, has_side_effects=True, vmem_limit_bytes=56 << 20),
        name="gram_sum",
    )(x, lm)

HI = jax.lax.Precision.HIGHEST
F32 = jnp.float32

BLK = {}
n = 0
for i in range(4):
    for j in range(i, 4):
        BLK[i, j] = n; n += 1

def mm(a, b):
    return lax.dot_general(a, b, (((1,), (0,)), ((), ())), precision=HI, preferred_element_type=F32)
def mtm(a, b):
    return lax.dot_general(a, b, (((0,), (0,)), ((), ())), precision=HI, preferred_element_type=F32)

def lane_splat(v, c):
    return jnp.broadcast_to(v[:, c:c + 1], (8, 128))
def row_splat(v, r):
    return jnp.broadcast_to(v[r:r + 1, :], (8, 128))

def tsum(xs):
    xs = list(xs)
    while len(xs) > 1:
        xs = [xs[i] + xs[i + 1] if i + 1 < len(xs) else xs[i] for i in range(0, len(xs), 2)]
    return xs[0]

def small_factor(a):
    l = [[None] * 8 for _ in range(8)]
    s = [None] * 8
    for j in range(8):
        s[j] = lax.rsqrt(a[j][j])
        for i in range(j + 1, 8):
            l[i][j] = a[i][j] * s[j]
        for i in range(j + 1, 8):
            for k in range(j + 1, i + 1):
                a[i][k] = a[i][k] - l[i][j] * l[k][j]
    w = [[None] * 8 for _ in range(8)]
    for j in range(8):
        w[j][j] = s[j]
        for i in range(j + 1, 8):
            w[i][j] = -s[i] * tsum([l[i][k] * w[k][j] for k in range(j, i)])
    return w

def diag_inverse(A):
    lane = lax.broadcasted_iota(jnp.int32, (8, 128), 1)
    sub = lax.broadcasted_iota(jnp.int32, (8, 128), 0)
    A = list(A)
    out = []
    for p in range(16):
        c0 = 8 * p
        P = A[p]
        cols = [lane_splat(P, c0 + j) for j in range(8)]
        a = [[row_splat(cols[j], i) if j <= i else None for j in range(8)] for i in range(8)]
        w = small_factor(a)
        inpanel = (lane >= c0) & (lane < c0 + 8)
        T = jnp.where(inpanel, (lane - c0 == sub).astype(F32), P)
        Tb = [row_splat(T, j) for j in range(8)]
        V = [tsum([w[i][j] * Tb[j] for j in range(i + 1)]) for i in range(8)]
        packed = V[0]
        for i in range(1, 8):
            packed = jnp.where(sub == i, V[i], packed)
        out.append(packed)
        if p < 15:
            Y = [tsum([w[i][j] * V[i] for i in range(j, 8)]) for j in range(8)]
            for q in range(p + 1, 16):
                m = [lane_splat(A[q], c0 + j) for j in range(8)]
                base = jnp.where(inpanel, 0.0, A[q])
                A[q] = base - tsum([m[j] * Y[j] for j in range(8)])
    row = [jnp.where(lane <= sub + 8 * p, out[p], 0.0) for p in range(16)]
    return row

def chol_kernel(g_ref, r_ref, hi_ref, lo_ref):
    n_rows = 1.0 / 1048576.0
    A = {k: g_ref[128 * v:128 * v + 128, :] * n_rows for k, v in BLK.items()}
    X = {}
    Bt = {}
    for k in range(4):
        strips = diag_inverse([A[k, k][8 * p:8 * p + 8, :] for p in range(16)])
        W = jnp.concatenate(strips, axis=0)
        U = {j: mm(W, A[k, j]) for j in range(k, 4)}
        for j in range(k + 1, 4):
            for i in range(k + 1, j + 1):
                A[i, j] = A[i, j] - mtm(U[i], U[j])
        X[k, k] = W
        for m in range(k):
            X[k, m] = mm(W, Bt[k, m])
        for i in range(k + 1, 4):
            for m in range(k + 1):
                t = mtm(U[i], X[k, m])
                Bt[i, m] = -t if m == k else Bt[i, m] - t
        rr = lax.broadcasted_iota(jnp.int32, (128, 128), 0)
        cc = lax.broadcasted_iota(jnp.int32, (128, 128), 1)
        for j in range(4):
            blk = jnp.zeros((128, 128), F32) if j < k else (jnp.where(rr <= cc, U[k], 0.0) if j == k else U[j])
            r_ref[128 * k:128 * k + 128, 128 * j:128 * j + 128] = blk
        for m in range(4):
            blk = X[k, m].T if m <= k else jnp.zeros((128, 128), F32)
            h = blk.astype(jnp.bfloat16)
            hi_ref[128 * m:128 * m + 128, 128 * k:128 * k + 128] = h
            lo_ref[128 * m:128 * m + 128, 128 * k:128 * k + 128] = (blk - h.astype(F32)).astype(jnp.bfloat16)

def chol(g):
    V = pl.BlockSpec(memory_space=pltpu.VMEM)
    return pl.pallas_call(chol_kernel,
        out_shape=(jax.ShapeDtypeStruct((512, 512), F32), jax.ShapeDtypeStruct((512, 512), jnp.bfloat16), jax.ShapeDtypeStruct((512, 512), jnp.bfloat16)),
        in_specs=[V], out_specs=(V, V, V),
        compiler_params=pltpu.CompilerParams(vmem_limit_bytes=56 << 20), name="factor")(g)

F32 = jnp.float32
def dot(a, b):
    return lax.dot_general(a, b, (((1,), (0,)), ((), ())), preferred_element_type=F32)

def q_kernel(hi_ref, lo_ref, rh_ref, rl_ref, q_ref):
    hi = hi_ref[...]
    lo = lo_ref[...]
    rh = rh_ref[...]
    rl = rl_ref[...]
    q_ref[:, :256] = dot(hi[:, :256], rh[:256, :256]) + (dot(hi[:, :256], rl[:256, :256]) + dot(lo[:, :256], rh[:256, :256]))
    q_ref[:, 256:] = dot(hi, rh[:, 256:]) + (dot(hi, rl[:, 256:]) + dot(lo, rh[:, 256:]))

def qmul(hi, lo, rh, rl, tile=1024):
    rows = hi.shape[0]
    row = pl.BlockSpec((tile, 512), lambda i: (i, 0))
    whole = pl.BlockSpec((512, 512), lambda i: (0, 0))
    return pl.pallas_call(q_kernel, grid=(rows // tile,), in_specs=[row, row, whole, whole], out_specs=row,
        out_shape=jax.ShapeDtypeStruct((rows, 512), F32),
        compiler_params=pltpu.CompilerParams(vmem_limit_bytes=56 << 20), name="q_product")(hi, lo, rh, rl)


def local(images, landmarks):
    summed, hi, lo = gram_sum(images, landmarks)
    r, rh, rl = chol(summed)
    return qmul(hi, lo, rh, rl, 1024), r


def solution(mesh):
    in_specs = (P("dp", None), P())
    out_specs = (P("dp", None), P())
    return jax.shard_map(local, mesh=mesh, in_specs=in_specs, out_specs=out_specs, check_vma=False)
```

```python
import functools
import math

import jax
import jax.numpy as jnp
from jax import lax
from jax.experimental import pallas as pl
from jax.experimental.pallas import tpu as pltpu
from jax.sharding import PartitionSpec as P

F32 = jnp.float32
BF = jnp.bfloat16
EPS = 1e-5
HI = lax.Precision.HIGHEST
MESH = pl.DeviceIdType.MESH
NX, NY, NZ = 4, 4, 8
NXY = NX * NY
TILES = 4
CHUNKS = (512, 768)

def dot_t(a, b, precision=None):
    return lax.dot_general(a, b, (((1,), (1,)), ((), ())), precision=precision, preferred_element_type=F32)

def t_dot(a, b):
    return lax.dot_general(a, b, (((0,), (0,)), ((), ())), preferred_element_type=F32)

def dev(y, z, x, c):
    return ((y * NZ + z) * NX + x) * 2 + c

def gram_kernel(x_ref, lm_ref, o_ref, hi_ref, lo_ref, xbuf, hbuf, lbuf, g_ref, acc0, acc2,
                crecv, half, rsbuf, zbuf, part, x_s, h_s, l_s,
                c_ss, c_rs, rs_ss, rs_rs, z_ss, z_rs, ag_ss, ag_rs, f_ss, f_rs):
    me = lax.axis_index("dp")
    c = me % 2
    x = (me // 2) % NX
    z = (me // (2 * NX)) % NZ
    y = me // (2 * NX * NZ)
    sib = dev(y, z, x, 1 - c)
    tile = x_ref.shape[0] // TILES

    def xy_peer(rel):
        px = (x + rel % NX) % NX
        py = (y + rel // NX) % NY
        return py * NX + px, dev(py, z, px, c)

    def xy_from(rel):
        px = (x + NX - rel % NX) % NX
        py = (y + NY - rel // NX) % NY
        return py * NX + px

    def z_peer(rel):
        return dev(y, (z + rel) % NZ, x, c)

    def sl(off, n):
        return pl.ds(pl.multiple_of(off, 8), n)

    def rows(t):
        return pl.ds(t * tile, tile)

    def x_copy(t):
        return pltpu.make_async_copy(x_ref.at[rows(t)], xbuf.at[rows(t)], x_s.at[t])

    def h_copy(t):
        return pltpu.make_async_copy(hbuf.at[rows(t)], hi_ref.at[rows(t)], h_s.at[t])

    def l_copy(t):
        return pltpu.make_async_copy(lbuf.at[rows(t)], lo_ref.at[rows(t)], l_s.at[t])

    for t in range(TILES):
        x_copy(t).start()

    bar = pltpu.get_barrier_semaphore()

    def sig(d):
        pl.semaphore_signal(bar, inc=1, device_id=(d,), device_id_type=MESH)

    sig(sib)

    @pl.loop(1, NXY)
    def _(r):
        sig(xy_peer(r)[1])

    @pl.loop(1, NZ)
    def _(r):
        sig(z_peer(r))

    lf = lm_ref[...].astype(F32)
    ones = jnp.full((8, lf.shape[1]), 1.0 / lf.shape[1], F32)
    ls = lax.rsqrt(dot_t(ones, lf * lf, HI) + EPS)[0:1, :] * (math.log2(math.e) / math.sqrt(lf.shape[1]))

    def features(t):
        xt = xbuf[rows(t), :]
        xf = xt.astype(F32)
        rs = lax.rsqrt(jnp.mean(xf * xf, axis=1, keepdims=True) + EPS)
        k = jnp.exp2(dot_t(xt, lm_ref[...]) * rs * ls)
        hi = k.astype(BF)
        hbuf[rows(t), :] = hi
        lbuf[rows(t), :] = (k - hi.astype(F32)).astype(BF)

    def gram0(t):
        hi = hbuf[rows(t), :]
        lo = lbuf[rows(t), :]
        p0 = t_dot(hi[:, :256], jnp.concatenate([hi, lo], axis=1))
        p2 = t_dot(lo[:, :256], hi[:, 256:])
        if t == 0:
            acc0[...] = p0
            acc2[...] = p2
        else:
            acc0[...] += p0
            acc2[...] += p2

    for t in range(TILES + 1):
        if t < TILES:
            x_copy(t).wait()
            features(t)
        if t > 0:
            h_copy(t - 1).start()
            l_copy(t - 1).start()
            gram0(t - 1)

    def put(n, b):
        g_ref[128 * n:128 * n + 128, :] = b

    cross = acc0[:, 512:768]
    g00 = acc0[:, :256] + (cross + cross.T)
    g01 = acc0[:, 256:512] + (acc0[:, 768:] + acc2[...])
    put(0, g00[:128, :128])
    put(1, g00[:128, 128:])
    put(2, g01[:128, :128])
    put(3, g01[:128, 128:])

    mine = y * NX + x
    C = []
    off = 0
    for k, n in enumerate(CHUNKS):
        C.append((k, off, n // 2, n // 32, off // 2, off // 32))
        off += n

    def core_copy(k, off, h, p, ho, po):
        return pltpu.make_async_remote_copy(
            g_ref.at[sl(off + (1 - c) * h, h)], crecv.at[pl.ds(ho, h)],
            c_ss.at[k], c_rs.at[k], device_id=(sib,), device_id_type=MESH)

    def rs_copy(ch, rel):
        k, off, h, p, ho, po = ch
        idx, d = xy_peer(rel)
        return pltpu.make_async_remote_copy(
            half.at[sl(ho + idx * p, p)], rsbuf.at[sl(ho + rel * p, p)],
            rs_ss.at[k, rel], rs_rs.at[k, rel], device_id=(d,), device_id_type=MESH)

    def z_copy(ch, rel):
        k, off, h, p, ho, po = ch
        return pltpu.make_async_remote_copy(
            part.at[pl.ds(po, p)], zbuf.at[z, pl.ds(po, p)],
            z_ss.at[k, rel], z_rs.at[k, rel], device_id=(z_peer(rel),), device_id_type=MESH)

    def ag_copy(ch, rel):
        k, off, h, p, ho, po = ch
        idx, d = xy_peer(rel)
        src = o_ref.at[sl(off + c * h + mine * p, p)]
        return pltpu.make_async_remote_copy(
            src, src, ag_ss.at[k, rel], ag_rs.at[k, rel], device_id=(d,), device_id_type=MESH)

    def fwd_copy(ch, rel, core):
        k, off, h, p, ho, po = ch
        src = o_ref.at[sl(off + core * h + xy_from(rel) * p, p)]
        return pltpu.make_async_remote_copy(
            src, src, f_ss.at[k, rel], f_rs.at[k, rel], device_id=(sib,), device_id_type=MESH)

    pl.semaphore_wait(bar, 1 + NXY - 1 + NZ - 1)
    core_copy(*C[0]).start()

    put(4, g00[128:, 128:])
    put(5, g01[128:, :128])
    put(6, g01[128:, 128:])
    h1 = hbuf[:, 256:]
    p1 = t_dot(h1, jnp.concatenate([h1, lbuf[:, 256:]], axis=1))
    cross = p1[:, 256:]
    g11 = p1[:, :256] + (cross + cross.T)
    put(7, g11[:128, :128])
    put(8, g11[:128, 128:])
    put(9, g11[128:, 128:])
    core_copy(*C[1]).start()

    for ch in C:
        k, off, h, p, ho, po = ch
        core_copy(*ch).wait_recv()
        half[pl.ds(ho, h)] = g_ref[sl(off + c * h, h)] + crecv[pl.ds(ho, h)]
        for r in range(1, NXY):
            rs_copy(ch, r).start()
    for ch in C:
        k, off, h, p, ho, po = ch

        @pl.loop(1, NXY)
        def _(r):
            rs_copy(ch, r).wait_recv()

        acc = half[sl(ho + mine * p, p)]
        for r in range(1, NXY):
            acc = acc + rsbuf[pl.ds(ho + r * p, p)]
        part[pl.ds(po, p)] = acc
        zbuf[z, pl.ds(po, p)] = acc
        for r in range(1, NZ):
            z_copy(ch, r).start()
    for ch in C:
        k, off, h, p, ho, po = ch

        @pl.loop(1, NZ)
        def _(r):
            z_copy(ch, r).wait_recv()

        acc = zbuf[0, pl.ds(po, p)]
        for r in range(1, NZ):
            acc = acc + zbuf[r, pl.ds(po, p)]
        o_ref[sl(off + c * h + mine * p, p)] = acc
        for r in range(1, NXY):
            ag_copy(ch, r).start()
        fwd_copy(ch, 0, c).start()
    for ch in C:
        @pl.loop(1, NXY)
        def _(r):
            ag_copy(ch, r).wait_recv()
            fwd_copy(ch, r, c).start()
    for ch in C:
        @pl.loop(0, NXY)
        def _(r):
            fwd_copy(ch, r, 1 - c).wait_recv()
    for ch in C:
        core_copy(*ch).wait_send()
        fwd_copy(ch, 0, c).wait_send()

        @pl.loop(1, NXY)
        def _(r):
            rs_copy(ch, r).wait_send()
            ag_copy(ch, r).wait_send()
            fwd_copy(ch, r, c).wait_send()

        @pl.loop(1, NZ)
        def _(r):
            z_copy(ch, r).wait_send()
    for t in range(TILES):
        h_copy(t).wait()
        l_copy(t).wait()

def gram_sum(x, lm):
    rows = x.shape[0]
    g = sum(CHUNKS)
    nc = len(CHUNKS)
    D = pltpu.SemaphoreType.DMA
    VM = pltpu.VMEM
    return pl.pallas_call(
        gram_kernel,
        out_shape=(jax.ShapeDtypeStruct((g, 128), F32), jax.ShapeDtypeStruct((rows, 512), BF), jax.ShapeDtypeStruct((rows, 512), BF)),
        in_specs=[pl.BlockSpec(memory_space=pl.ANY), pl.BlockSpec(memory_space=VM)],
        out_specs=(pl.BlockSpec(memory_space=VM), pl.BlockSpec(memory_space=pl.ANY), pl.BlockSpec(memory_space=pl.ANY)),
        scratch_shapes=[
            VM((rows, 256), BF), VM((rows, 512), BF), VM((rows, 512), BF), VM((g, 128), F32),
            VM((256, 1024), F32), VM((256, 256), F32),
            VM((g // 2, 128), F32), VM((g // 2, 128), F32), VM((g // 2, 128), F32),
            VM((NZ, g // 32, 128), F32), VM((g // 32, 128), F32),
            D((TILES,)), D((TILES,)), D((TILES,)),
            D((nc,)), D((nc,)), D((nc, NXY)), D((nc, NXY)), D((nc, NZ)), D((nc, NZ)),
            D((nc, NXY)), D((nc, NXY)), D((nc, NXY)), D((nc, NXY)),
        ],
        compiler_params=pltpu.CompilerParams(collective_id=0, has_side_effects=True, vmem_limit_bytes=56 << 20),
        name="gram_sum",
    )(x, lm)

F32 = jnp.float32
HI = lax.Precision.HIGHEST

def mm(a, b):
    return lax.dot_general(a, b, (((1,), (0,)), ((), ())), precision=HI, preferred_element_type=F32)

def mtm(a, b):
    return lax.dot_general(a, b, (((0,), (0,)), ((), ())), precision=HI, preferred_element_type=F32)

def lane_splat(v, c):
    return jnp.broadcast_to(v[:, c:c + 1], (8, 128))

def row_splat(v, r):
    return jnp.broadcast_to(v[r:r + 1, :], (8, 128))

def tsum(xs):
    xs = list(xs)
    while len(xs) > 1:
        xs = [xs[i] + xs[i + 1] if i + 1 < len(xs) else xs[i] for i in range(0, len(xs), 2)]
    return xs[0]

def diag_inverse(A, between=lambda: None):
    lane = lax.broadcasted_iota(jnp.int32, (8, 128), 1)
    sub = lax.broadcasted_iota(jnp.int32, (8, 128), 0)
    A = list(A)
    out = []
    cols = [lane_splat(A[0], j) for j in range(8)]
    for p in range(16):
        c0 = 8 * p
        last = p == 15
        inpanel = (lane >= c0) & (lane < c0 + 8)
        if not last:
            mk = [lane_splat(A[p + 1], c0 + j) for j in range(8)]
            raw = list(mk)
            nxt = [lane_splat(A[p + 1], c0 + 8 + j) for j in range(8)]
        D = cols
        Wc = [None] * 8
        r = [None] * 8
        piv = [None] * 8
        for j in range(8):
            piv[j] = row_splat(D[j], j)
            r[j] = 1.0 / piv[j]
            f = D[j] * r[j]
            e = [row_splat(D[j], k) for k in range(8)]
            for k in range(j + 1, 8):
                D[k] = D[k] - f * e[k]
            if not last:
                f2 = mk[j] * r[j]
                for k in range(j + 1, 8):
                    mk[k] = mk[k] - f2 * e[k]
                for k in range(8):
                    nxt[k] = nxt[k] - f2 * row_splat(mk[j], k)
            fm = jnp.where(sub > j, f, 0.0)
            for k in range(j):
                Wc[k] = Wc[k] - fm * row_splat(Wc[k], j)
            Wc[j] = jnp.where(sub == j, 1.0, -fm)
        pv = piv[0]
        for i in range(1, 8):
            pv = jnp.where(sub == i, piv[i], pv)
        T = jnp.where(inpanel, (lane - c0 == sub).astype(F32), A[p])
        V = tsum([Wc[j] * row_splat(T, j) for j in range(8)])
        out.append(jnp.where(lane <= sub + c0, V * lax.rsqrt(pv), 0.0))
        if not last:
            Vb = [row_splat(V, s) * r[s] for s in range(8)]
            Y = [tsum([Vb[k]] + [row_splat(Wc[k], s) * Vb[s] for s in range(k + 1, 8)]) for k in range(8)]
            for q in range(p + 1, 16):
                m = raw if q == p + 1 else [lane_splat(A[q], c0 + j) for j in range(8)]
                base = jnp.where(inpanel, 0.0, A[q])
                A[q] = base - tsum([m[j] * Y[j] for j in range(8)])
            cols = nxt
        between()
    return out

QT = 512
QS = 128

def factor_kernel(g_ref, hi_ref, lo_ref, q_ref, r_ref, hb, lb, qb, rb, rh, rl, in_s, q0_s, q1_s, r_s):
    rows = hi_ref.shape[0]
    nt = rows // QT

    def loads(t):
        s = pl.ds(t * QT, QT)
        return (pltpu.make_async_copy(hi_ref.at[s], hb.at[s], in_s.at[0, t]),
                pltpu.make_async_copy(lo_ref.at[s], lb.at[s], in_s.at[1, t]))

    def q_out(t, half, sem):
        s = pl.ds(t * QT, QT)
        cols = pl.ds(256 * half, 256)
        return pltpu.make_async_copy(qb.at[s, cols], q_ref.at[s, cols], sem.at[t])

    def r_out(k):
        s = pl.ds(128 * k, 128)
        return pltpu.make_async_copy(rb.at[s], r_ref.at[s], r_s.at[k])

    for t in range(nt):
        for cp in loads(t):
            cp.start()

    order = [(i, j) for i in range(4) for j in range(i, 4)]
    A = {ij: g_ref[128 * n:128 * n + 128, :] * (1.0 / 1048576.0) for n, ij in enumerate(order)}
    U, X, B = {}, {}, {}
    rr = lax.broadcasted_iota(jnp.int32, (128, 128), 0)
    cc = lax.broadcasted_iota(jnp.int32, (128, 128), 1)
    zero = jnp.zeros((128, 128), F32)
    cat = jnp.concatenate

    def put_inverse(k, m):
        blk = X[k, m].T
        h = blk.astype(jnp.bfloat16)
        at = (slice(128 * m, 128 * m + 128), slice(128 * k, 128 * k + 128))
        rh[at] = h
        rl[at] = (blk - h.astype(F32)).astype(jnp.bfloat16)

    def row_rest(k):
        if k < 2:
            w = mm(X[k, k], cat([A[k, j] for j in range(k + 2, 4)], axis=1))
            for n, j in enumerate(range(k + 2, 4)):
                U[k, j] = w[:, 128 * n:128 * n + 128]

    def row_store(k):
        U[k, k] = jnp.where(rr <= cc, mm(X[k, k], A[k, k]), 0.0)
        for j in range(4):
            rb[128 * k:128 * k + 128, 128 * j:128 * j + 128] = U[k, j] if j >= k else zero
        r_out(k).start()

    def update(k, i, js):
        w = mtm(U[k, i], cat([U[k, j] for j in js], axis=1))
        for n, j in enumerate(js):
            A[i, j] = A[i, j] - w[:, 128 * n:128 * n + 128]

    def inverse_row(k):
        if k > 0:
            w = mm(X[k, k], cat([B[k, m] for m in range(k)], axis=1))
            for m in range(k):
                X[k, m] = w[:, 128 * m:128 * m + 128]

    def inverse_update(k, i):
        w = mtm(U[k, i], cat([X[k, m] for m in range(k + 1)], axis=1))
        for m in range(k + 1):
            t = w[:, 128 * m:128 * m + 128]
            B[i, m] = -t if m == k else B[i, m] - t

    def weights(half):
        n = 256 * (half + 1)
        cols = slice(256 * half, 256 * half + 256)
        h = rh[:n, cols]
        return cat([h, rl[:n, cols], h], axis=0)

    def product(row, size, half, w):
        n = 256 * (half + 1)
        s = slice(row, row + size)
        h = hb[s, :n]
        qb[s, 256 * half:256 * half + 256] = lax.dot_general(
            cat([h, h, lb[s, :n]], axis=1), w, (((1,), (0,)), ((), ())), preferred_element_type=F32)

    tasks = []
    rate = [1]

    def between():
        for _ in range(rate[0]):
            if tasks:
                tasks.pop(0)()

    def drain():
        while tasks:
            tasks.pop(0)()

    def q_task(row):
        product(row, QS, 0, W0[0])
        if (row + QS) % QT == 0:
            q_out(row // QT, 0, q0_s).start()

    W0 = []
    Pt = functools.partial
    first_q = []
    for k in range(4):
        strips = diag_inverse([A[k, k][8 * p:8 * p + 8, :] for p in range(16)], between)
        if k < 2:
            drain()
        X[k, k] = cat(strips, axis=0)
        if k < 3:
            U[k, k + 1] = mm(X[k, k], A[k, k + 1])
            update(k, k + 1, [k + 1])
        new = []
        if k < 3:
            if k < 2:
                new.append(Pt(row_rest, k))
            for i in range(k + 1, 4):
                js = [j for j in range(i, 4) if (i, j) != (k + 1, k + 1)]
                if js:
                    new.append(Pt(update, k, i, js))
        new.append(Pt(inverse_row, k))
        for i in range(k + 1, 4):
            new.append(Pt(inverse_update, k, i))
        for m in range(k + 1):
            new.append(Pt(put_inverse, k, m))
        new.append(Pt(row_store, k))
        if k < 3:
            if k == 1:
                for f in new:
                    f()
                rh[256:, :256] = jnp.zeros((256, 256), jnp.bfloat16)
                rl[256:, :256] = jnp.zeros((256, 256), jnp.bfloat16)
                rh[128:256, :128] = jnp.zeros((128, 128), jnp.bfloat16)
                rl[128:256, :128] = jnp.zeros((128, 128), jnp.bfloat16)
                rh[384:, 256:384] = jnp.zeros((128, 128), jnp.bfloat16)
                rl[384:, 256:384] = jnp.zeros((128, 128), jnp.bfloat16)
                for t in range(nt):
                    for cp in loads(t):
                        cp.wait()
                W0.append(weights(0))
                first_q = [Pt(q_task, s) for s in range(0, rows, QS)]
                tasks.extend(first_q)
            elif k == 2:
                tasks[0:0] = new
                rate[0] = 2
            else:
                tasks.extend(new)
        else:
            drain()
            for f in new:
                f()
    w = weights(1)
    for t in range(nt):
        product(t * QT, QT, 1, w)
        q_out(t, 1, q1_s).start()
    for t in range(nt):
        q_out(t, 0, q0_s).wait()
        q_out(t, 1, q1_s).wait()
    for k in range(4):
        r_out(k).wait()

def factor_q(g, hi, lo):
    rows = hi.shape[0]
    V = pltpu.VMEM
    D = pltpu.SemaphoreType.DMA
    nt = rows // QT
    BF16 = jnp.bfloat16
    anym = pl.BlockSpec(memory_space=pl.ANY)
    return pl.pallas_call(
        factor_kernel,
        out_shape=(jax.ShapeDtypeStruct((rows, 512), F32), jax.ShapeDtypeStruct((512, 512), F32)),
        in_specs=[pl.BlockSpec(memory_space=V), anym, anym], out_specs=(anym, anym),
        scratch_shapes=[V((rows, 512), BF16), V((rows, 512), BF16), V((rows, 512), F32), V((512, 512), F32),
                        V((512, 512), BF16), V((512, 512), BF16), D((2, nt)), D((nt,)), D((nt,)), D((4,))],
        compiler_params=pltpu.CompilerParams(vmem_limit_bytes=56 << 20), name="factor_q")(g, hi, lo)


def local(images, landmarks):
    summed, hi, lo = gram_sum(images, landmarks)
    return factor_q(summed, hi, lo)


def solution(mesh):
    in_specs = (P("dp", None), P())
    out_specs = (P("dp", None), P())
    return jax.shard_map(local, mesh=mesh, in_specs=in_specs, out_specs=out_specs, check_vma=False)
```

```python
import functools
import math

import jax
import jax.numpy as jnp
from jax import lax
from jax.experimental import pallas as pl
from jax.experimental.pallas import tpu as pltpu
from jax.sharding import PartitionSpec as P

F32 = jnp.float32
HI = lax.Precision.HIGHEST

def mm(a, b):
    return lax.dot_general(a, b, (((1,), (0,)), ((), ())), precision=HI, preferred_element_type=F32)

def mtm(a, b):
    return lax.dot_general(a, b, (((0,), (0,)), ((), ())), precision=HI, preferred_element_type=F32)

def lane_splat(v, c):
    return jnp.broadcast_to(v[:, c:c + 1], (8, 128))

def row_splat(v, r):
    return jnp.broadcast_to(v[r:r + 1, :], (8, 128))

def tsum(xs):
    xs = list(xs)
    while len(xs) > 1:
        xs = [xs[i] + xs[i + 1] if i + 1 < len(xs) else xs[i] for i in range(0, len(xs), 2)]
    return xs[0]

def diag_inverse(A, between=lambda: None):
    lane = lax.broadcasted_iota(jnp.int32, (8, 128), 1)
    sub = lax.broadcasted_iota(jnp.int32, (8, 128), 0)
    A = list(A)
    out = []
    cols = [lane_splat(A[0], j) for j in range(8)]
    for p in range(16):
        c0 = 8 * p
        last = p == 15
        inpanel = (lane >= c0) & (lane < c0 + 8)
        if not last:
            mk = [lane_splat(A[p + 1], c0 + j) for j in range(8)]
            raw = list(mk)
            nxt = [lane_splat(A[p + 1], c0 + 8 + j) for j in range(8)]
        D = cols
        Wc = [None] * 8
        r = [None] * 8
        piv = [None] * 8
        for j in range(8):
            piv[j] = row_splat(D[j], j)
            r[j] = 1.0 / piv[j]
            f = D[j] * r[j]
            e = [row_splat(D[j], k) for k in range(8)]
            for k in range(j + 1, 8):
                D[k] = D[k] - f * e[k]
            if not last:
                f2 = mk[j] * r[j]
                for k in range(j + 1, 8):
                    mk[k] = mk[k] - f2 * e[k]
                for k in range(8):
                    nxt[k] = nxt[k] - f2 * row_splat(mk[j], k)
            fm = jnp.where(sub > j, f, 0.0)
            for k in range(j):
                Wc[k] = Wc[k] - fm * row_splat(Wc[k], j)
            Wc[j] = jnp.where(sub == j, 1.0, -fm)
        pv = piv[0]
        for i in range(1, 8):
            pv = jnp.where(sub == i, piv[i], pv)
        T = jnp.where(inpanel, (lane - c0 == sub).astype(F32), A[p])
        V = tsum([Wc[j] * row_splat(T, j) for j in range(8)])
        out.append(jnp.where(lane <= sub + c0, V * lax.rsqrt(pv), 0.0))
        if not last:
            Vb = [row_splat(V, s) * r[s] for s in range(8)]
            Y = [tsum([Vb[k]] + [row_splat(Wc[k], s) * Vb[s] for s in range(k + 1, 8)]) for k in range(8)]
            for q in range(p + 1, 16):
                m = raw if q == p + 1 else [lane_splat(A[q], c0 + j) for j in range(8)]
                base = jnp.where(inpanel, 0.0, A[q])
                A[q] = base - tsum([m[j] * Y[j] for j in range(8)])
            cols = nxt
        between()
    return out

F32 = jnp.float32
BF = jnp.bfloat16
EPS = 1e-5
HI = lax.Precision.HIGHEST
MESH = pl.DeviceIdType.MESH
NX, NY, NZ = 4, 4, 8
NXY = NX * NY
TILES = 8
CHUNKS = (512, 768)

def dot_t(a, b, precision=None):
    return lax.dot_general(a, b, (((1,), (1,)), ((), ())), precision=precision, preferred_element_type=F32)

def t_dot(a, b):
    return lax.dot_general(a, b, (((0,), (0,)), ((), ())), preferred_element_type=F32)

def dev(y, z, x, c):
    return ((y * NZ + z) * NX + x) * 2 + c

def gram_kernel(x_ref, l_ref, o_ref, w_ref, hi_ref, lo_ref, lm_ref, xbuf, hbuf, lbuf, g_ref, acc0, acc2,
                crecv, half, rsbuf, zbuf, part, lm_s, x_s, h_s, l_s,
                c_ss, c_rs, rs_ss, rs_rs, z_ss, z_rs, ag_ss, ag_rs, f_ss, f_rs):
    me = lax.axis_index("dp")
    c = me % 2
    x = (me // 2) % NX
    z = (me // (2 * NX)) % NZ
    y = me // (2 * NX * NZ)
    sib = dev(y, z, x, 1 - c)
    tile = x_ref.shape[0] // TILES

    def xy_peer(rel):
        px = (x + rel % NX) % NX
        py = (y + rel // NX) % NY
        return py * NX + px, dev(py, z, px, c)

    def xy_from(rel):
        px = (x + NX - rel % NX) % NX
        py = (y + NY - rel // NX) % NY
        return py * NX + px

    def z_peer(rel):
        return dev(y, (z + rel) % NZ, x, c)

    def sl(off, n):
        return pl.ds(pl.multiple_of(off, 8), n)

    def rows(t):
        return pl.ds(t * tile, tile)

    def x_copy(t):
        return pltpu.make_async_copy(x_ref.at[rows(t)], xbuf.at[rows(t)], x_s.at[t])

    def h_copy(t):
        return pltpu.make_async_copy(hbuf.at[rows(t)], hi_ref.at[rows(t)], h_s.at[t])

    def l_copy(t):
        return pltpu.make_async_copy(lbuf.at[rows(t)], lo_ref.at[rows(t)], l_s.at[t])

    lm_copy = pltpu.make_async_copy(l_ref, lm_ref, lm_s)
    lm_copy.start()
    for t in range(TILES):
        x_copy(t).start()

    bar = pltpu.get_barrier_semaphore()

    def sig(d):
        pl.semaphore_signal(bar, inc=1, device_id=(d,), device_id_type=MESH)

    sig(sib)

    @pl.loop(1, NXY)
    def _(r):
        sig(xy_peer(r)[1])

    @pl.loop(1, NZ)
    def _(r):
        sig(z_peer(r))

    lm_copy.wait()
    lf = lm_ref[...].astype(F32)
    sq = lf * lf
    sq_hi = sq.astype(BF)
    ones = jnp.full((8, lf.shape[1]), 1.0, BF)
    total = dot_t(ones, sq_hi) + dot_t(ones, (sq - sq_hi.astype(F32)).astype(BF))
    ls = lax.rsqrt(total / lf.shape[1] + EPS)[0:1, :] * (math.log2(math.e) / math.sqrt(lf.shape[1]))

    def features(t):
        xt = xbuf[rows(t), :]
        xf = xt.astype(F32)
        rs = lax.rsqrt(jnp.mean(xf * xf, axis=1, keepdims=True) + EPS)
        k = jnp.exp2(dot_t(xt, lm_ref[...]) * rs * ls)
        hi = k.astype(BF)
        hbuf[rows(t), :] = hi
        lbuf[rows(t), :] = (k - hi.astype(F32)).astype(BF)

    def gram0(t):
        hi = hbuf[rows(t), :]
        lo = lbuf[rows(t), :]
        p0 = t_dot(hi[:, :256], jnp.concatenate([hi, lo], axis=1))
        p2 = t_dot(lo[:, :256], hi[:, 256:])
        if t == 0:
            acc0[...] = p0
            acc2[...] = p2
        else:
            acc0[...] += p0
            acc2[...] += p2

    for t in range(TILES + 1):
        if t < TILES:
            x_copy(t).wait()
            features(t)
        if t > 0:
            h_copy(t - 1).start()
            l_copy(t - 1).start()
            gram0(t - 1)

    def put(n, b):
        g_ref[128 * n:128 * n + 128, :] = b

    cross = acc0[:, 512:768]
    g00 = acc0[:, :256] + (cross + cross.T)
    g01 = acc0[:, 256:512] + (acc0[:, 768:] + acc2[...])
    put(0, g00[:128, :128])
    put(1, g00[:128, 128:])
    put(2, g01[:128, :128])
    put(3, g01[:128, 128:])

    mine = y * NX + x
    C = []
    off = 0
    for k, n in enumerate(CHUNKS):
        C.append((k, off, n // 2, n // 32, off // 2, off // 32))
        off += n

    def core_copy(k, off, h, p, ho, po):
        return pltpu.make_async_remote_copy(
            g_ref.at[sl(off + (1 - c) * h, h)], crecv.at[pl.ds(ho, h)],
            c_ss.at[k], c_rs.at[k], device_id=(sib,), device_id_type=MESH)

    def rs_copy(ch, rel):
        k, off, h, p, ho, po = ch
        idx, d = xy_peer(rel)
        return pltpu.make_async_remote_copy(
            half.at[sl(ho + idx * p, p)], rsbuf.at[sl(ho + rel * p, p)],
            rs_ss.at[k, rel], rs_rs.at[k, rel], device_id=(d,), device_id_type=MESH)

    def z_copy(ch, rel):
        k, off, h, p, ho, po = ch
        return pltpu.make_async_remote_copy(
            part.at[pl.ds(po, p)], zbuf.at[z, pl.ds(po, p)],
            z_ss.at[k, rel], z_rs.at[k, rel], device_id=(z_peer(rel),), device_id_type=MESH)

    def ag_copy(ch, rel):
        k, off, h, p, ho, po = ch
        idx, d = xy_peer(rel)
        src = o_ref.at[sl(off + c * h + mine * p, p)]
        return pltpu.make_async_remote_copy(
            src, src, ag_ss.at[k, rel], ag_rs.at[k, rel], device_id=(d,), device_id_type=MESH)

    def fwd_copy(ch, rel, core):
        k, off, h, p, ho, po = ch
        src = o_ref.at[sl(off + core * h + xy_from(rel) * p, p)]
        return pltpu.make_async_remote_copy(
            src, src, f_ss.at[k, rel], f_rs.at[k, rel], device_id=(sib,), device_id_type=MESH)

    pl.semaphore_wait(bar, 1 + NXY - 1 + NZ - 1)
    core_copy(*C[0]).start()

    put(4, g00[128:, 128:])
    put(5, g01[128:, :128])
    put(6, g01[128:, 128:])
    h1 = hbuf[:, 256:]
    p1 = t_dot(h1, jnp.concatenate([h1, lbuf[:, 256:]], axis=1))
    cross = p1[:, 256:]
    g11 = p1[:, :256] + (cross + cross.T)
    put(7, g11[:128, :128])
    put(8, g11[:128, 128:])
    put(9, g11[128:, 128:])
    core_copy(*C[1]).start()

    for ch in C:
        k, off, h, p, ho, po = ch
        core_copy(*ch).wait_recv()
        half[pl.ds(ho, h)] = g_ref[sl(off + c * h, h)] + crecv[pl.ds(ho, h)]
        for r in range(1, NXY):
            rs_copy(ch, r).start()
    for ch in C:
        k, off, h, p, ho, po = ch

        @pl.loop(1, NXY)
        def _(r):
            rs_copy(ch, r).wait_recv()

        acc = half[sl(ho + mine * p, p)]
        for r in range(1, NXY):
            acc = acc + rsbuf[pl.ds(ho + r * p, p)]
        part[pl.ds(po, p)] = acc
        zbuf[z, pl.ds(po, p)] = acc
        for r in range(1, NZ):
            z_copy(ch, r).start()
    for ch in C:
        k, off, h, p, ho, po = ch

        @pl.loop(1, NZ)
        def _(r):
            z_copy(ch, r).wait_recv()

        acc = zbuf[0, pl.ds(po, p)]
        for r in range(1, NZ):
            acc = acc + zbuf[r, pl.ds(po, p)]
        o_ref[sl(off + c * h + mine * p, p)] = acc
        for r in range(1, NXY):
            ag_copy(ch, r).start()
        fwd_copy(ch, 0, c).start()
    @pl.loop(1, NXY)
    def _(r):
        ag_copy(C[0], r).wait_recv()
        fwd_copy(C[0], r, c).start()

    @pl.loop(0, NXY)
    def _(r):
        fwd_copy(C[0], r, 1 - c).wait_recv()

    pending = list(range(1, NXY))
    panels = [0]

    def between():
        panels[0] += 1
        while pending and panels[0] >= 8 and len(pending) > 2 * (15 - panels[0]):
            r = pending.pop(0)
            ag_copy(C[1], r).wait_recv()
            fwd_copy(C[1], r, c).start()

    first = o_ref[:128, :] * (1.0 / 1048576.0)
    w_ref[...] = jnp.concatenate(diag_inverse([first[8 * p:8 * p + 8, :] for p in range(16)], between), axis=0)

    @pl.loop(0, NXY)
    def _(r):
        fwd_copy(C[1], r, 1 - c).wait_recv()

    for ch in C:
        core_copy(*ch).wait_send()
        fwd_copy(ch, 0, c).wait_send()

        @pl.loop(1, NXY)
        def _(r):
            rs_copy(ch, r).wait_send()
            ag_copy(ch, r).wait_send()
            fwd_copy(ch, r, c).wait_send()

        @pl.loop(1, NZ)
        def _(r):
            z_copy(ch, r).wait_send()
    for t in range(TILES):
        h_copy(t).wait()
        l_copy(t).wait()

def gram_sum(x, lm):
    rows = x.shape[0]
    g = sum(CHUNKS)
    nc = len(CHUNKS)
    D = pltpu.SemaphoreType.DMA
    VM = pltpu.VMEM
    return pl.pallas_call(
        gram_kernel,
        out_shape=(jax.ShapeDtypeStruct((g, 128), F32), jax.ShapeDtypeStruct((128, 128), F32), jax.ShapeDtypeStruct((rows, 512), BF), jax.ShapeDtypeStruct((rows, 512), BF)),
        in_specs=[pl.BlockSpec(memory_space=pl.ANY), pl.BlockSpec(memory_space=pl.ANY)],
        out_specs=(pl.BlockSpec(memory_space=VM), pl.BlockSpec(memory_space=VM), pl.BlockSpec(memory_space=pl.ANY), pl.BlockSpec(memory_space=pl.ANY)),
        scratch_shapes=[
            VM((512, 256), BF), VM((rows, 256), BF), VM((rows, 512), BF), VM((rows, 512), BF), VM((g, 128), F32),
            VM((256, 1024), F32), VM((256, 256), F32),
            VM((g // 2, 128), F32), VM((g // 2, 128), F32), VM((g // 2, 128), F32),
            VM((NZ, g // 32, 128), F32), VM((g // 32, 128), F32),
            D, D((TILES,)), D((TILES,)), D((TILES,)),
            D((nc,)), D((nc,)), D((nc, NXY)), D((nc, NXY)), D((nc, NZ)), D((nc, NZ)),
            D((nc, NXY)), D((nc, NXY)), D((nc, NXY)), D((nc, NXY)),
        ],
        compiler_params=pltpu.CompilerParams(collective_id=0, has_side_effects=True, vmem_limit_bytes=56 << 20),
        name="gram_sum",
    )(x, lm)

QT = 512
QS = 128

def factor_kernel(g_ref, w_ref, hi_ref, lo_ref, q_ref, r_ref, hb, lb, qb, rb, zh, zl, w01, w23, w3, in_s, q_s, r_s):
    rows = hi_ref.shape[0]
    nt = rows // QT

    def loads(t):
        s = pl.ds(t * QT, QT)
        return (pltpu.make_async_copy(hi_ref.at[s], hb.at[s], in_s.at[0, t]),
                pltpu.make_async_copy(lo_ref.at[s], lb.at[s], in_s.at[1, t]))

    def q_out(t, part):
        s = pl.ds(t * QT, QT)
        cols = pl.ds((0, 256, 384)[part], (256, 128, 128)[part])
        return pltpu.make_async_copy(qb.at[s, cols], q_ref.at[s, cols], q_s.at[part, t])

    def r_out(k):
        s = pl.ds(128 * k, 128)
        return pltpu.make_async_copy(rb.at[s], r_ref.at[s], r_s.at[k])

    for t in range(nt):
        for cp in loads(t):
            cp.start()

    order = [(i, j) for i in range(4) for j in range(i, 4)]
    A = {ij: g_ref[128 * n:128 * n + 128, :] * (1.0 / 1048576.0) for n, ij in enumerate(order)}
    U, X, B = {}, {}, {}
    rr = lax.broadcasted_iota(jnp.int32, (128, 128), 0)
    cc = lax.broadcasted_iota(jnp.int32, (128, 128), 1)
    zero = jnp.zeros((128, 128), F32)
    cat = jnp.concatenate

    def split(blk):
        h = blk.astype(jnp.bfloat16)
        return h, (blk - h.astype(F32)).astype(jnp.bfloat16)

    def put(w, part, m, col, blk):
        h, l = split(blk)
        c = slice(col, col + 128)
        for n, v in enumerate((h, l, h)):
            w[n * part + 128 * m:n * part + 128 * m + 128, c] = v

    def row_rest(k):
        if k < 2:
            w = mm(X[k, k], cat([A[k, j] for j in range(k + 2, 4)], axis=1))
            for n, j in enumerate(range(k + 2, 4)):
                U[k, j] = w[:, 128 * n:128 * n + 128]

    def row_store(k):
        U[k, k] = jnp.where(rr <= cc, mm(X[k, k], A[k, k]), 0.0)
        for j in range(4):
            rb[128 * k:128 * k + 128, 128 * j:128 * j + 128] = U[k, j] if j >= k else zero
        r_out(k).start()

    def update(k, i, js):
        w = mtm(U[k, i], cat([U[k, j] for j in js], axis=1))
        for n, j in enumerate(js):
            A[i, j] = A[i, j] - w[:, 128 * n:128 * n + 128]

    def inverse_row(k):
        if k > 0:
            w = mm(X[k, k], cat([B[k, m] for m in range(k)], axis=1))
            for m in range(k):
                X[k, m] = w[:, 128 * m:128 * m + 128]

    def inverse_update(k, i):
        w = mtm(U[k, i], cat([X[k, m] for m in range(k + 1)], axis=1))
        for m in range(k + 1):
            t = w[:, 128 * m:128 * m + 128]
            B[i, m] = -t if m == k else B[i, m] - t

    def left(s, n):
        h = hb[s, :n]
        return cat([h, h, lb[s, :n]], axis=1)

    def dot(a, w):
        return lax.dot_general(a, w, (((1,), (0,)), ((), ())), preferred_element_type=F32)

    def done(row, part):
        if (row + QS) % QT == 0:
            q_out(row // QT, part).start()

    def q01(row):
        s = slice(row, row + QS)
        qb[s, :256] = dot(left(s, 256), w01[...])
        done(row, 0)

    def q2(row):
        s = slice(row, row + QS)
        w = dot(left(s, 384), w23[...])
        qb[s, 256:384] = w[:, :128]
        zh[s], zl[s] = split(w[:, 128:] + (hb[s, 384:].astype(F32) + lb[s, 384:].astype(F32)))
        done(row, 1)

    def q3(t):
        s = slice(t * QT, t * QT + QT)
        h = zh[s]
        qb[s, 384:] = dot(cat([h, h, zl[s]], axis=1), w3[...])
        q_out(t, 2).start()

    tasks = []
    plan = [0, 0]

    def between():
        plan[0] += 1
        while tasks and len(tasks) * 16 > plan[1] * (16 - plan[0]):
            tasks.pop(0)()

    def wait_loads():
        for t in range(nt):
            for cp in loads(t):
                cp.wait()

    def zeros():
        for n in range(3):
            w01[256 * n + 128:256 * n + 256, :128] = jnp.zeros((128, 128), jnp.bfloat16)

    Pt = functools.partial
    for k in range(4):
        plan[:] = [0, len(tasks)]
        if k == 0:
            X[0, 0] = w_ref[...]
        else:
            X[k, k] = cat(diag_inverse([A[k, k][8 * p:8 * p + 8, :] for p in range(16)], between), axis=0)
        if k < 3:
            U[k, k + 1] = mm(X[k, k], A[k, k + 1])
            update(k, k + 1, [k + 1])
        else:
            put(w3, 128, 0, 0, X[3, 3].T)
        if k < 2:
            tasks.append(Pt(row_rest, k))
        for i in range(k + 1, 4):
            js = [j for j in range(i, 4) if (i, j) != (k + 1, k + 1)]
            if js:
                tasks.append(Pt(update, k, i, js))
        if k < 3:
            tasks.append(Pt(inverse_row, k))
        for i in range(k + 1, 4):
            tasks.append(Pt(inverse_update, k, i))
        if k == 1:
            tasks.append(zeros)
            for i in range(2):
                for m in range(i + 1):
                    tasks.append(lambda i=i, m=m: put(w01, 256, m, 128 * i, X[i, m].T))
            tasks.append(wait_loads)
            tasks += [Pt(q01, s) for s in range(0, rows, QS)]
        if k == 2:
            for m in range(3):
                tasks.append(lambda m=m: put(w23, 384, m, 0, X[2, m].T))
                tasks.append(lambda m=m: put(w23, 384, m, 128, B[3, m].T))
            tasks += [Pt(q2, s) for s in range(0, rows, QS)]
        tasks.insert(len(tasks) if k < 2 else 0, Pt(row_store, k))
        if k == 3:
            for t in range(nt):
                q3(t)
            tasks.pop(0)()
    for part in range(3):
        for t in range(nt):
            q_out(t, part).wait()
    for k in range(4):
        r_out(k).wait()

def factor_q(g, w0, hi, lo):
    rows = hi.shape[0]
    V = pltpu.VMEM
    D = pltpu.SemaphoreType.DMA
    nt = rows // QT
    BF16 = jnp.bfloat16
    anym = pl.BlockSpec(memory_space=pl.ANY)
    return pl.pallas_call(
        factor_kernel,
        out_shape=(jax.ShapeDtypeStruct((rows, 512), F32), jax.ShapeDtypeStruct((512, 512), F32)),
        in_specs=[pl.BlockSpec(memory_space=V), pl.BlockSpec(memory_space=V), anym, anym], out_specs=(anym, anym),
        scratch_shapes=[V((rows, 512), BF16), V((rows, 512), BF16), V((rows, 512), F32), V((512, 512), F32),
                        V((rows, 128), BF16), V((rows, 128), BF16), V((768, 256), BF16), V((1152, 256), BF16), V((384, 128), BF16),
                        D((2, nt)), D((3, nt)), D((4,))],
        compiler_params=pltpu.CompilerParams(vmem_limit_bytes=56 << 20), name="factor_q")(g, w0, hi, lo)


def local(images, landmarks):
    summed, w0, hi, lo = gram_sum(images, landmarks)
    return factor_q(summed, w0, hi, lo)


def solution(mesh):
    in_specs = (P("dp", None), P())
    out_specs = (P("dp", None), P())
    return jax.shard_map(local, mesh=mesh, in_specs=in_specs, out_specs=out_specs, check_vma=False)
```

```python
import functools
import math

import jax
import jax.numpy as jnp
from jax import lax
from jax.experimental import pallas as pl
from jax.experimental.pallas import tpu as pltpu
from jax.sharding import PartitionSpec as P

F32 = jnp.float32
HI = lax.Precision.HIGHEST

def mm(a, b):
    return lax.dot_general(a, b, (((1,), (0,)), ((), ())), precision=HI, preferred_element_type=F32)

def mtm(a, b):
    return lax.dot_general(a, b, (((0,), (0,)), ((), ())), precision=HI, preferred_element_type=F32)

def lane_splat(v, c):
    return jnp.broadcast_to(v[:, c:c + 1], (8, 128))

def row_splat(v, r):
    return jnp.broadcast_to(v[r:r + 1, :], (8, 128))

def tsum(xs):
    xs = list(xs)
    while len(xs) > 1:
        xs = [xs[i] + xs[i + 1] if i + 1 < len(xs) else xs[i] for i in range(0, len(xs), 2)]
    return xs[0]

def diag_inverse(A, between=lambda: None):
    lane = lax.broadcasted_iota(jnp.int32, (8, 128), 1)
    sub = lax.broadcasted_iota(jnp.int32, (8, 128), 0)
    A = list(A)
    out = []
    cols = [lane_splat(A[0], j) for j in range(8)]
    for p in range(16):
        c0 = 8 * p
        last = p == 15
        inpanel = (lane >= c0) & (lane < c0 + 8)
        if not last:
            mk = [lane_splat(A[p + 1], c0 + j) for j in range(8)]
            raw = list(mk)
            nxt = [lane_splat(A[p + 1], c0 + 8 + j) for j in range(8)]
        D = cols
        Wc = [None] * 8
        r = [None] * 8
        piv = [None] * 8
        for j in range(8):
            piv[j] = row_splat(D[j], j)
            r[j] = 1.0 / piv[j]
            f = D[j] * r[j]
            e = [row_splat(D[j], k) for k in range(8)]
            for k in range(j + 1, 8):
                D[k] = D[k] - f * e[k]
            if not last:
                f2 = mk[j] * r[j]
                for k in range(j + 1, 8):
                    mk[k] = mk[k] - f2 * e[k]
                for k in range(8):
                    nxt[k] = nxt[k] - f2 * row_splat(mk[j], k)
            fm = jnp.where(sub > j, f, 0.0)
            for k in range(j):
                Wc[k] = Wc[k] - fm * row_splat(Wc[k], j)
            Wc[j] = jnp.where(sub == j, 1.0, -fm)
        pv = piv[0]
        for i in range(1, 8):
            pv = jnp.where(sub == i, piv[i], pv)
        T = jnp.where(inpanel, (lane - c0 == sub).astype(F32), A[p])
        V = tsum([Wc[j] * row_splat(T, j) for j in range(8)])
        out.append(jnp.where(lane <= sub + c0, V * lax.rsqrt(pv), 0.0))
        if not last:
            Vb = [row_splat(V, s) * r[s] for s in range(8)]
            Y = [tsum([Vb[k]] + [row_splat(Wc[k], s) * Vb[s] for s in range(k + 1, 8)]) for k in range(8)]
            for q in range(p + 1, 16):
                m = raw if q == p + 1 else [lane_splat(A[q], c0 + j) for j in range(8)]
                base = jnp.where(inpanel, 0.0, A[q])
                A[q] = base - tsum([m[j] * Y[j] for j in range(8)])
            cols = nxt
        between()
    return out

F32 = jnp.float32
BF = jnp.bfloat16
EPS = 1e-5
HI = lax.Precision.HIGHEST
MESH = pl.DeviceIdType.MESH
NX, NY, NZ = 4, 4, 8
NXY = NX * NY
TILES = 8
CHUNKS = (512, 768)

def dot_t(a, b, precision=None):
    return lax.dot_general(a, b, (((1,), (1,)), ((), ())), precision=precision, preferred_element_type=F32)

def t_dot(a, b):
    return lax.dot_general(a, b, (((0,), (0,)), ((), ())), preferred_element_type=F32)

def dev(y, z, x, c):
    return ((y * NZ + z) * NX + x) * 2 + c

def gram_kernel(x_ref, l_ref, o_ref, w_ref, hi_ref, lo_ref, lm_ref, xbuf, hbuf, lbuf, g_ref, acc0, acc2,
                crecv, half, rsbuf, zbuf, part, lm_s, x_s, h_s, l_s,
                c_ss, c_rs, rs_ss, rs_rs, z_ss, z_rs, ag_ss, ag_rs, f_ss, f_rs):
    me = lax.axis_index("dp")
    c = me % 2
    x = (me // 2) % NX
    z = (me // (2 * NX)) % NZ
    y = me // (2 * NX * NZ)
    sib = dev(y, z, x, 1 - c)
    tile = x_ref.shape[0] // TILES

    def xy_peer(rel):
        px = (x + rel % NX) % NX
        py = (y + rel // NX) % NY
        return py * NX + px, dev(py, z, px, c)

    def xy_from(rel):
        px = (x + NX - rel % NX) % NX
        py = (y + NY - rel // NX) % NY
        return py * NX + px

    def z_peer(rel):
        return dev(y, (z + rel) % NZ, x, c)

    def sl(off, n):
        return pl.ds(pl.multiple_of(off, 8), n)

    def rows(t):
        return pl.ds(t * tile, tile)

    def x_copy(t):
        return pltpu.make_async_copy(x_ref.at[rows(t)], xbuf.at[rows(t)], x_s.at[t])

    def h_copy(t):
        return pltpu.make_async_copy(hbuf.at[rows(t)], hi_ref.at[rows(t)], h_s.at[t])

    def l_copy(t):
        return pltpu.make_async_copy(lbuf.at[rows(t)], lo_ref.at[rows(t)], l_s.at[t])

    lm_copy = pltpu.make_async_copy(l_ref, lm_ref, lm_s)
    lm_copy.start()
    for t in range(TILES):
        x_copy(t).start()

    bar = pltpu.get_barrier_semaphore()

    def sig(d):
        pl.semaphore_signal(bar, inc=1, device_id=(d,), device_id_type=MESH)

    sig(sib)

    @pl.loop(1, NXY)
    def _(r):
        sig(xy_peer(r)[1])

    @pl.loop(1, NZ)
    def _(r):
        sig(z_peer(r))

    lm_copy.wait()
    lf = lm_ref[...].astype(F32)
    sq = lf * lf
    sq_hi = sq.astype(BF)
    ones = jnp.full((8, lf.shape[1]), 1.0, BF)
    total = dot_t(ones, sq_hi) + dot_t(ones, (sq - sq_hi.astype(F32)).astype(BF))
    ls = lax.rsqrt(total / lf.shape[1] + EPS)[0:1, :] * (math.log2(math.e) / math.sqrt(lf.shape[1]))

    def features(t):
        xt = xbuf[rows(t), :]
        xf = xt.astype(F32)
        rs = lax.rsqrt(jnp.mean(xf * xf, axis=1, keepdims=True) + EPS)
        k = jnp.exp2(dot_t(xt, lm_ref[...]) * rs * ls)
        hi = k.astype(BF)
        hbuf[rows(t), :] = hi
        lbuf[rows(t), :] = (k - hi.astype(F32)).astype(BF)

    def gram0(t):
        hi = hbuf[rows(t), :]
        lo = lbuf[rows(t), :]
        p0 = t_dot(hi[:, :256], jnp.concatenate([hi, lo], axis=1))
        p2 = t_dot(lo[:, :256], hi[:, 256:])
        if t == 0:
            acc0[...] = p0
            acc2[...] = p2
        else:
            acc0[...] += p0
            acc2[...] += p2

    for t in range(TILES + 1):
        if t < TILES:
            x_copy(t).wait()
            features(t)
        if t > 0:
            h_copy(t - 1).start()
            l_copy(t - 1).start()
            gram0(t - 1)

    def put(n, b):
        g_ref[128 * n:128 * n + 128, :] = b

    cross = acc0[:, 512:768]
    g00 = acc0[:, :256] + (cross + cross.T)
    g01 = acc0[:, 256:512] + (acc0[:, 768:] + acc2[...])
    put(0, g00[:128, :128])
    put(1, g00[:128, 128:])
    put(2, g01[:128, :128])
    put(3, g01[:128, 128:])

    mine = y * NX + x
    C = []
    off = 0
    for k, n in enumerate(CHUNKS):
        C.append((k, off, n // 2, n // 32, off // 2, off // 32))
        off += n

    def core_copy(k, off, h, p, ho, po):
        return pltpu.make_async_remote_copy(
            g_ref.at[sl(off + (1 - c) * h, h)], crecv.at[pl.ds(ho, h)],
            c_ss.at[k], c_rs.at[k], device_id=(sib,), device_id_type=MESH)

    def rs_copy(ch, rel):
        k, off, h, p, ho, po = ch
        idx, d = xy_peer(rel)
        return pltpu.make_async_remote_copy(
            half.at[sl(ho + idx * p, p)], rsbuf.at[sl(ho + rel * p, p)],
            rs_ss.at[k, rel], rs_rs.at[k, rel], device_id=(d,), device_id_type=MESH)

    def z_copy(ch, rel):
        k, off, h, p, ho, po = ch
        return pltpu.make_async_remote_copy(
            part.at[pl.ds(po, p)], zbuf.at[z, pl.ds(po, p)],
            z_ss.at[k, rel], z_rs.at[k, rel], device_id=(z_peer(rel),), device_id_type=MESH)

    def ag_copy(ch, rel):
        k, off, h, p, ho, po = ch
        idx, d = xy_peer(rel)
        src = o_ref.at[sl(off + c * h + mine * p, p)]
        return pltpu.make_async_remote_copy(
            src, src, ag_ss.at[k, rel], ag_rs.at[k, rel], device_id=(d,), device_id_type=MESH)

    def fwd_copy(ch, rel, core):
        k, off, h, p, ho, po = ch
        src = o_ref.at[sl(off + core * h + xy_from(rel) * p, p)]
        return pltpu.make_async_remote_copy(
            src, src, f_ss.at[k, rel], f_rs.at[k, rel], device_id=(sib,), device_id_type=MESH)

    pl.semaphore_wait(bar, 1 + NXY - 1 + NZ - 1)
    core_copy(*C[0]).start()

    put(4, g00[128:, 128:])
    put(5, g01[128:, :128])
    put(6, g01[128:, 128:])
    h1 = hbuf[:, 256:]
    p1 = t_dot(h1, jnp.concatenate([h1, lbuf[:, 256:]], axis=1))
    cross = p1[:, 256:]
    g11 = p1[:, :256] + (cross + cross.T)
    put(7, g11[:128, :128])
    put(8, g11[:128, 128:])
    put(9, g11[128:, 128:])
    core_copy(*C[1]).start()

    for ch in C:
        k, off, h, p, ho, po = ch
        core_copy(*ch).wait_recv()
        half[pl.ds(ho, h)] = g_ref[sl(off + c * h, h)] + crecv[pl.ds(ho, h)]
        for r in range(1, NXY):
            rs_copy(ch, r).start()
    for ch in C:
        k, off, h, p, ho, po = ch

        @pl.loop(1, NXY)
        def _(r):
            rs_copy(ch, r).wait_recv()

        acc = half[sl(ho + mine * p, p)]
        for r in range(1, NXY):
            acc = acc + rsbuf[pl.ds(ho + r * p, p)]
        part[pl.ds(po, p)] = acc
        zbuf[z, pl.ds(po, p)] = acc
        for r in range(1, NZ):
            z_copy(ch, r).start()
    for ch in C:
        k, off, h, p, ho, po = ch

        @pl.loop(1, NZ)
        def _(r):
            z_copy(ch, r).wait_recv()

        acc = zbuf[0, pl.ds(po, p)]
        for r in range(1, NZ):
            acc = acc + zbuf[r, pl.ds(po, p)]
        o_ref[sl(off + c * h + mine * p, p)] = acc
        for r in range(1, NXY):
            ag_copy(ch, r).start()
        fwd_copy(ch, 0, c).start()
    for r in (1, 3, 4, 12, 2, 5, 7, 8, 13, 15, 6, 9, 11, 14, 10):
        ag_copy(C[0], r).wait_recv()
        fwd_copy(C[0], r, c).start()
    for r in range(NXY):
        fwd_copy(C[0], r, 1 - c).wait_recv()

    pending = list(range(1, NXY))
    panels = [0]

    def between():
        panels[0] += 1
        while pending and panels[0] >= 8 and len(pending) > 2 * (15 - panels[0]):
            r = pending.pop(0)
            ag_copy(C[1], r).wait_recv()
            fwd_copy(C[1], r, c).start()

    first = o_ref[:128, :] * (1.0 / 1048576.0)
    w_ref[...] = jnp.concatenate(diag_inverse([first[8 * p:8 * p + 8, :] for p in range(16)], between), axis=0)

    @pl.loop(0, NXY)
    def _(r):
        fwd_copy(C[1], r, 1 - c).wait_recv()

    for ch in C:
        core_copy(*ch).wait_send()
        fwd_copy(ch, 0, c).wait_send()

        @pl.loop(1, NXY)
        def _(r):
            rs_copy(ch, r).wait_send()
            ag_copy(ch, r).wait_send()
            fwd_copy(ch, r, c).wait_send()

        @pl.loop(1, NZ)
        def _(r):
            z_copy(ch, r).wait_send()
    for t in range(TILES):
        h_copy(t).wait()
        l_copy(t).wait()

def gram_sum(x, lm):
    rows = x.shape[0]
    g = sum(CHUNKS)
    nc = len(CHUNKS)
    D = pltpu.SemaphoreType.DMA
    VM = pltpu.VMEM
    return pl.pallas_call(
        gram_kernel,
        out_shape=(jax.ShapeDtypeStruct((g, 128), F32), jax.ShapeDtypeStruct((128, 128), F32), jax.ShapeDtypeStruct((rows, 512), BF), jax.ShapeDtypeStruct((rows, 512), BF)),
        in_specs=[pl.BlockSpec(memory_space=pl.ANY), pl.BlockSpec(memory_space=pl.ANY)],
        out_specs=(pl.BlockSpec(memory_space=VM), pl.BlockSpec(memory_space=VM), pl.BlockSpec(memory_space=pl.ANY), pl.BlockSpec(memory_space=pl.ANY)),
        scratch_shapes=[
            VM((512, 256), BF), VM((rows, 256), BF), VM((rows, 512), BF), VM((rows, 512), BF), VM((g, 128), F32),
            VM((256, 1024), F32), VM((256, 256), F32),
            VM((g // 2, 128), F32), VM((g // 2, 128), F32), VM((g // 2, 128), F32),
            VM((NZ, g // 32, 128), F32), VM((g // 32, 128), F32),
            D, D((TILES,)), D((TILES,)), D((TILES,)),
            D((nc,)), D((nc,)), D((nc, NXY)), D((nc, NXY)), D((nc, NZ)), D((nc, NZ)),
            D((nc, NXY)), D((nc, NXY)), D((nc, NXY)), D((nc, NXY)),
        ],
        compiler_params=pltpu.CompilerParams(collective_id=0, has_side_effects=True, vmem_limit_bytes=56 << 20),
        name="gram_sum",
    )(x, lm)

QT = 512
QS = 128

def factor_kernel(g_ref, w_ref, hi_ref, lo_ref, q_ref, r_ref, hb, lb, qb, rb, zh, zl, zh2, zl2, z3, w01, w23, w3, in_s, q_s, r_s):
    rows = hi_ref.shape[0]
    nt = rows // QT

    def loads(t):
        s = pl.ds(t * QT, QT)
        return (pltpu.make_async_copy(hi_ref.at[s], hb.at[s], in_s.at[0, t]),
                pltpu.make_async_copy(lo_ref.at[s], lb.at[s], in_s.at[1, t]))

    def q_out(t, part):
        s = pl.ds(t * QT, QT)
        cols = pl.ds((0, 256, 384)[part], (256, 128, 128)[part])
        return pltpu.make_async_copy(qb.at[s, cols], q_ref.at[s, cols], q_s.at[part, t])

    def r_out(k):
        s = pl.ds(128 * k, 128)
        return pltpu.make_async_copy(rb.at[s], r_ref.at[s], r_s.at[k])

    for t in range(nt):
        for cp in loads(t):
            cp.start()

    order = [(i, j) for i in range(4) for j in range(i, 4)]
    A = {ij: g_ref[128 * n:128 * n + 128, :] * (1.0 / 1048576.0) for n, ij in enumerate(order)}
    U, X, B = {}, {}, {}
    rr = lax.broadcasted_iota(jnp.int32, (128, 128), 0)
    cc = lax.broadcasted_iota(jnp.int32, (128, 128), 1)
    zero = jnp.zeros((128, 128), F32)
    cat = jnp.concatenate

    def split(blk):
        h = blk.astype(jnp.bfloat16)
        return h, (blk - h.astype(F32)).astype(jnp.bfloat16)

    def put(w, part, m, col, blk):
        h, l = split(blk)
        c = slice(col, col + 128)
        for n, v in enumerate((h, l, h)):
            w[n * part + 128 * m:n * part + 128 * m + 128, c] = v

    def row_rest(k):
        if k < 2:
            w = mm(X[k, k], cat([A[k, j] for j in range(k + 2, 4)], axis=1))
            for n, j in enumerate(range(k + 2, 4)):
                U[k, j] = w[:, 128 * n:128 * n + 128]

    def row_store(k):
        U[k, k] = jnp.where(rr <= cc, mm(X[k, k], A[k, k]), 0.0)
        for j in range(4):
            rb[128 * k:128 * k + 128, 128 * j:128 * j + 128] = U[k, j] if j >= k else zero
        r_out(k).start()

    def update(k, i, js):
        w = mtm(U[k, i], cat([U[k, j] for j in js], axis=1))
        for n, j in enumerate(js):
            A[i, j] = A[i, j] - w[:, 128 * n:128 * n + 128]

    def inverse_row(k):
        if k > 0:
            w = mm(X[k, k], cat([B[k, m] for m in range(k)], axis=1))
            for m in range(k):
                X[k, m] = w[:, 128 * m:128 * m + 128]

    def inverse_update(k, i):
        w = mtm(U[k, i], cat([X[k, m] for m in range(k + 1)], axis=1))
        for m in range(k + 1):
            t = w[:, 128 * m:128 * m + 128]
            B[i, m] = -t if m == k else B[i, m] - t

    def left(s, n):
        h = hb[s, :n]
        return cat([h, h, lb[s, :n]], axis=1)

    def dot(a, w):
        return lax.dot_general(a, w, (((1,), (0,)), ((), ())), preferred_element_type=F32)

    def done(row, part):
        if (row + QS) % QT == 0:
            q_out(row // QT, part).start()

    def q01(row):
        s = slice(row, row + QS)
        w = dot(left(s, 256), w01[...])
        qb[s, :256] = w[:, :256]
        rest = w[:, 256:] + (hb[s, 256:].astype(F32) + lb[s, 256:].astype(F32))
        zh2[s], zl2[s] = split(rest[:, :128])
        z3[s] = rest[:, 128:]
        done(row, 0)

    def q2(row):
        s = slice(row, row + QS)
        h = zh2[s]
        w = dot(cat([h, h, zl2[s]], axis=1), w23[...])
        qb[s, 256:384] = w[:, :128]
        zh[s], zl[s] = split(z3[s] + w[:, 128:])
        done(row, 1)

    def q3(t):
        s = slice(t * QT, t * QT + QT)
        h = zh[s]
        qb[s, 384:] = dot(cat([h, h, zl[s]], axis=1), w3[...])
        q_out(t, 2).start()

    tasks = []
    plan = [0, 0]

    def between():
        plan[0] += 1
        while tasks and len(tasks) * 16 > plan[1] * (16 - plan[0]):
            tasks.pop(0)()

    def wait_loads():
        for t in range(nt):
            for cp in loads(t):
                cp.wait()

    def zeros():
        for n in range(3):
            w01[256 * n + 128:256 * n + 256, :128] = jnp.zeros((128, 128), jnp.bfloat16)

    Pt = functools.partial
    for k in range(4):
        plan[:] = [0, len(tasks)]
        if k == 0:
            X[0, 0] = w_ref[...]
        else:
            X[k, k] = cat(diag_inverse([A[k, k][8 * p:8 * p + 8, :] for p in range(16)], between), axis=0)
        if k < 3:
            U[k, k + 1] = mm(X[k, k], A[k, k + 1])
            update(k, k + 1, [k + 1])
        else:
            put(w3, 128, 0, 0, X[3, 3].T)
        if k < 2:
            tasks.append(Pt(row_rest, k))
        for i in range(k + 1, 4):
            js = [j for j in range(i, 4) if (i, j) != (k + 1, k + 1)]
            if js:
                tasks.append(Pt(update, k, i, js))
        if k < 2:
            tasks.append(Pt(inverse_row, k))
            for i in range(k + 1, 4):
                tasks.append(Pt(inverse_update, k, i))
        if k == 1:
            tasks.append(zeros)
            for i in range(2):
                for m in range(i + 1):
                    tasks.append(lambda i=i, m=m: put(w01, 256, m, 128 * i, X[i, m].T))
            for i in range(2, 4):
                for m in range(2):
                    tasks.append(lambda i=i, m=m: put(w01, 256, m, 128 * i, B[i, m].T))
            tasks.append(wait_loads)
            tasks += [Pt(q01, s) for s in range(0, rows, QS)]
        if k == 2:
            put(w23, 128, 0, 0, X[2, 2].T)
            put(w23, 128, 0, 128, -mtm(U[2, 3], X[2, 2]).T)
            tasks += [Pt(q2, s) for s in range(0, rows, QS)]
        tasks.insert(len(tasks) if k < 2 else 0, Pt(row_store, k))
        if k == 3:
            for t in range(nt):
                q3(t)
            tasks.pop(0)()
    for part in range(3):
        for t in range(nt):
            q_out(t, part).wait()
    for k in range(4):
        r_out(k).wait()

def factor_q(g, w0, hi, lo):
    rows = hi.shape[0]
    V = pltpu.VMEM
    D = pltpu.SemaphoreType.DMA
    nt = rows // QT
    BF16 = jnp.bfloat16
    anym = pl.BlockSpec(memory_space=pl.ANY)
    return pl.pallas_call(
        factor_kernel,
        out_shape=(jax.ShapeDtypeStruct((rows, 512), F32), jax.ShapeDtypeStruct((512, 512), F32)),
        in_specs=[pl.BlockSpec(memory_space=V), pl.BlockSpec(memory_space=V), anym, anym], out_specs=(anym, anym),
        scratch_shapes=[V((rows, 512), BF16), V((rows, 512), BF16), V((rows, 512), F32), V((512, 512), F32),
                        V((rows, 128), BF16), V((rows, 128), BF16), V((rows, 128), BF16), V((rows, 128), BF16), V((rows, 128), F32),
                        V((768, 512), BF16), V((384, 256), BF16), V((384, 128), BF16),
                        D((2, nt)), D((3, nt)), D((4,))],
        compiler_params=pltpu.CompilerParams(vmem_limit_bytes=56 << 20), name="factor_q")(g, w0, hi, lo)


def local(images, landmarks):
    summed, w0, hi, lo = gram_sum(images, landmarks)
    return factor_q(summed, w0, hi, lo)


def solution(mesh):
    in_specs = (P("dp", None), P())
    out_specs = (P("dp", None), P())
    return jax.shard_map(local, mesh=mesh, in_specs=in_specs, out_specs=out_specs, check_vma=False)
```
